128 devices in a mesh: rows: 8 (over z_hi, y), cols: 8 (over z_lo, x), rel: 2 (over core).
Axes of the slice: x: 4, y: 4, z: 4 (z_hi: 2, z_lo: 2; z = z_hi * 2 + z_lo), core: 2. Of those that a mesh axis runs over, the one named last changes fastest.
Arguments:
- features: bfloat16 [32768, 512], P('cols', 'rows'), may hold values from -6 to 6
- rel_weight: bfloat16 [8, 512, 512], P('rel'), may hold values from -0.25 to 0.25
- self_weight: bfloat16 [512, 512], replicated, may hold values from -0.25 to 0.25
- bias: float32 [512], replicated, may hold values from -3 to 3
- block_code: int32 [8, 8, 2, 128], P('rows', 'cols', 'rel'), may hold values from 0 to 4095, as said below
- block_counts: int32 [8, 8, 2, 128, 128, 128], P('rows', 'cols', 'rel'), may hold values from 0 to 3, as said below
Outputs:
- node_out: bfloat16 [32768, 512], P(('rows', 'cols', 'rel'))
The draws below stay inside these ranges and needn't reach their ends.
Inputs may be any that keep to these rules, and one draw needn't show every extreme that they name: `block_code`: within one device the codes are distinct, each below 4096. `block_counts`: on each device the slots with counts come first, 128 // k of them for some k from 1 to 5; some device has all 128 slots in use; the other slots are all zero.
All inputs are finite; a program needn't handle non-finite values.
Results may differ from the reference program's by a relative error of at most 0.0036.
Values may be sent and summed in bfloat16 or wider, within the bound.
No kernel may reach another device: no remote copies, remote signals or barrier semaphores. Data moves between devices by JAX's collectives and lax.ppermute only.
A program may use at most 256 MiB of HBM per device.

```python
import jax
import jax.numpy as jnp
from jax import lax

D = 512
REL_DEV = 4
BLOCK = 128
BLK_GRP = 32
MAXB = 128
RELS = 8
NODES = 32768
N_ROWS = 8
N_COLS = 8
N_REL = 2


def slot_plan(key):
    devices_all = N_ROWS * N_COLS * N_REL
    total = REL_DEV * BLK_GRP * BLK_GRP
    keys = jax.random.split(jax.random.fold_in(key, 11), devices_all)
    codes = jax.vmap(lambda one_key: jax.random.permutation(one_key, total)[:MAXB])(keys).astype(jnp.int32)
    divisor = jax.random.randint(jax.random.fold_in(key, 12), (devices_all,), 1, 6)
    live = MAXB // divisor
    picked = jax.random.randint(jax.random.fold_in(key, 13), (), 0, devices_all)
    live = jnp.where(jnp.arange(devices_all) == picked, MAXB, live)
    return (codes, live, picked)


def draw_block_code(key, part):
    codes, live, picked = slot_plan(key)
    return codes.reshape(N_ROWS, N_COLS, N_REL, MAXB).astype(jnp.int32)


def draw_block_counts(key, part):
    codes, live, picked = slot_plan(key)
    key = jax.random.fold_in(key, 2)
    devices_all = N_ROWS * N_COLS * N_REL
    values = jax.random.randint(jax.random.fold_in(key, 21), (devices_all, MAXB, BLOCK, BLOCK), 1, 4)
    present = jax.random.randint(jax.random.fold_in(key, 22), (devices_all, MAXB, BLOCK, BLOCK), 0, 100) < 8
    values = values * present.astype(jnp.int32)
    used = (jnp.arange(MAXB)[None, :] < live[:, None]).astype(jnp.int32)
    values = values * used[:, :, None, None]
    values = values.at[picked, 0, 0, 0].set(3)
    return values.reshape(N_ROWS, N_COLS, N_REL, MAXB, BLOCK, BLOCK).astype(jnp.int32)


def steps_of(stream_key, extent, shards, smallest, largest):
    level, own = 1.0, jax.random.fold_in(stream_key, 6)
    for axis_at, shards_of in shards:
        steps = jnp.exp(jax.random.uniform(jax.random.fold_in(own, axis_at), (shards_of,), jnp.float32, smallest / len(shards), largest / len(shards)))
        level = level * jnp.repeat(steps, extent[axis_at] // shards_of).reshape([-1 if axis == axis_at else 1 for axis in range(len(extent))])
    return level


def noise(rng, shape, deviation, limit, cuts=(), kind=jnp.bfloat16):
    drawn = deviation * jax.random.normal(rng, shape, jnp.float32)
    if cuts:
        drawn = drawn * steps_of(rng, shape, cuts, -0.22, 0.18)
    return jnp.clip(drawn, -limit, limit).astype(kind)


def setup_inputs(seed: int = 0) -> dict:
    splits = jax.random.split(jax.random.key(seed), 7)
    return {
        "features": noise(splits[0], (NODES, D), 1.0, 6.0, ((0, 8), (1, 8))),
        "rel_weight": noise(splits[1], (RELS, D, D), D ** -0.5, 0.25, ((0, 2),)),
        "self_weight": noise(splits[2], (D, D), D ** -0.5, 0.25),
        "bias": noise(splits[3], (D,), 0.5, 3.0, (), jnp.float32),
        "block_code": draw_block_code(jax.random.fold_in(splits[6], 71), 0),
        "block_counts": draw_block_counts(jax.random.fold_in(splits[6], 71), 0),
    }


def reference(features, rel_weight, self_weight, bias, block_code, block_counts):
    nblk_all = NODES // BLOCK
    hidden = jnp.einsum('nk,rkd->rnd', features.astype(jnp.float32), rel_weight.astype(jnp.float32)).astype(jnp.bfloat16)
    hid_blocks = hidden.reshape(RELS, nblk_all, BLOCK, D)
    row_ids = jnp.arange(N_ROWS, dtype=jnp.int32)[:, None, None, None]
    col_ids = jnp.arange(N_COLS, dtype=jnp.int32)[None, :, None, None]
    grp_ids = jnp.arange(N_REL, dtype=jnp.int32)[None, None, :, None]
    relation = grp_ids * REL_DEV + block_code // (BLK_GRP * BLK_GRP)
    target = row_ids * BLK_GRP + (block_code // BLK_GRP) % BLK_GRP
    source = col_ids * BLK_GRP + block_code % BLK_GRP
    shape = (N_ROWS, N_COLS, N_REL, MAXB)
    relation = jnp.broadcast_to(relation, shape).reshape(-1, MAXB).astype(jnp.int32)
    target = jnp.broadcast_to(target, shape).reshape(-1, MAXB).astype(jnp.int32)
    source = jnp.broadcast_to(source, shape).reshape(-1, MAXB).astype(jnp.int32)
    counts = block_counts.reshape(-1, MAXB, BLOCK, BLOCK)
    rowsum = jnp.sum(counts, axis=-1).astype(jnp.float32)
    degree = jnp.zeros((RELS, nblk_all, BLOCK), jnp.float32).at[relation, target].add(rowsum)
    inverse = 1.0 / jnp.maximum(degree, 1.0)

    def one_device(total, items):
        cnt, rel_i, tgt_i, src_i = items
        weight = (cnt.astype(jnp.float32) * inverse[rel_i, tgt_i][:, :, None]).astype(jnp.bfloat16)
        source_rows = hid_blocks[rel_i, src_i]
        contrib = jnp.einsum('sij,sjd->sid', weight.astype(jnp.float32), source_rows.astype(jnp.float32))
        return total.at[tgt_i].add(contrib), None

    start = jnp.zeros((nblk_all, BLOCK, D), jnp.float32)
    aggregate, _ = lax.scan(one_device, start, (counts, relation, target, source))
    total = aggregate.reshape(NODES, D) + jnp.dot(features, self_weight, preferred_element_type=jnp.float32) + bias
    return jax.nn.relu(total).astype(jnp.bfloat16)
```

```python
import functools

import jax
import jax.numpy as jnp
from jax import lax
from jax.experimental import pallas as pl
from jax.experimental.pallas import tpu as pltpu
from jax.sharding import PartitionSpec as P

BLOCK = 128
WIDTH = 512
NBLK = 32
NREL = 4
SLOTS = 128
PIECE = 64
NODES = NBLK * BLOCK
CHUNK = 512
HSTEPS = NODES // CHUNK
TSTEP = 8
NT = (((1,), (1,)), ((), ()))
OFF_CORE = (((0, 1), (1, 1), (0, 2)), ((0, 3), (1, 3), (1, 0)))
OFF_BOTH = (1, 2)


def shifted(row, off, sign):
    return (row // 4 + off[0]) % 2 * 4 + (row % 4 + sign * off[1]) % 4


def piece_order(row, core):
    first = [jnp.where(core == 0, shifted(row, a, -1), shifted(row, b, -1)) for a, b in zip(*OFF_CORE)]
    second = [jnp.where(core == 0, shifted(row, b, -1), shifted(row, a, -1)) for a, b in zip(*OFF_CORE)]
    return jnp.stack([row] + first + second + [shifted(row, OFF_BOTH, -1)])


def degree_kernel(seg_ref, counts_ref, deg_ref):
    step = pl.program_id(0)

    @pl.when(step == 0)
    def _():
        deg_ref[...] = jnp.zeros_like(deg_ref)

    per = counts_ref.shape[0]
    ones = jnp.ones((8, BLOCK), jnp.bfloat16)
    for s in range(per):
        c = counts_ref[s].astype(jnp.float32).astype(jnp.bfloat16)
        row = lax.dot_general(ones, c, NT, preferred_element_type=jnp.float32)
        seg = seg_ref[step * per + s]
        deg_ref[pl.ds(seg, 1), :] += row[0:1]


def partial_degrees(segment, counts):
    per = 16
    return pl.pallas_call(
        degree_kernel,
        grid_spec=pltpu.PrefetchScalarGridSpec(
            num_scalar_prefetch=1,
            grid=(SLOTS // per,),
            in_specs=[pl.BlockSpec((per, BLOCK, BLOCK), lambda i, s: (i, 0, 0))],
            out_specs=pl.BlockSpec((SLOTS, BLOCK), lambda i, s: (0, 0)),
        ),
        out_shape=jax.ShapeDtypeStruct((NREL * NBLK, BLOCK), jnp.float32),
        cost_estimate=pl.CostEstimate(flops=2 * SLOTS * BLOCK * BLOCK * 8, bytes_accessed=SLOTS * BLOCK * BLOCK * 4, transcendentals=0),
        name="degrees",
    )(segment, counts)


def main_kernel(
    meta_ref, order_ref, starts_ref, codes_ref,
    p0, p1, p2, p3, p4, p5, p6, half_own, half_sib, wt_ref, deg_ref, counts_hbm,
    sib_ref, own_ref,
    hid, cnt, inv_t, acc, sem,
):
    step = pl.program_id(0)
    counts_copy = pltpu.make_async_copy(counts_hbm, cnt, sem)

    @pl.when(step == 0)
    def _():
        counts_copy.start()
        degree = deg_ref[0]
        for k in range(1, deg_ref.shape[0]):
            degree = degree + deg_ref[k]
        inv_t[...] = (1.0 / jnp.maximum(degree, 1.0)).T

    @pl.when(step < HSTEPS)
    def _():
        chunk = lax.rem(meta_ref[0] * (HSTEPS // 2) + step, HSTEPS)
        last = jnp.where(step < HSTEPS // 2, half_own[...], half_sib[...])
        x = jnp.concatenate([p[...] for p in (p0, p1, p2, p3, p4, p5, p6)] + [last], axis=0)

        def one(r, carry):
            h = jnp.dot(wt_ref[r], x, preferred_element_type=jnp.float32).astype(jnp.bfloat16)
            for b in range(CHUNK // BLOCK):
                hid[r, chunk * (CHUNK // BLOCK) + b] = h[:, b * BLOCK : (b + 1) * BLOCK]
            return carry

        lax.fori_loop(0, NREL, one, 0)

    @pl.when(step == HSTEPS)
    def _():
        counts_copy.wait()

    def weights(slot, live):
        code = codes_ref[slot]
        seg = lax.shift_right_logical(code, 5)
        rel = lax.shift_right_logical(code, 10)
        src = jnp.bitwise_and(code, NBLK - 1)
        scale = jnp.take_along_axis(inv_t[...], jnp.full((BLOCK, BLOCK), seg, jnp.int32), axis=1)
        w = cnt[slot].astype(jnp.float32) * scale
        if live is not None:
            w = jnp.where(live, w, 0.0)
        return hid[rel, src], w.astype(jnp.bfloat16)

    def targets(first, out_ref):
        for u in range(TSTEP):
            begin = starts_ref[first + u]
            end = starts_ref[first + u + 1]
            acc[...] = jnp.zeros_like(acc)

            def pair(q, carry):
                at = begin + 2 * q
                h1, w1 = weights(order_ref[at], None)
                h2, w2 = weights(order_ref[jnp.minimum(at + 1, SLOTS - 1)], at + 1 < end)
                h = jnp.concatenate([h1, h2], axis=1)
                w = jnp.concatenate([w1, w2], axis=1)
                acc[...] += lax.dot_general(h, w, NT, preferred_element_type=jnp.float32)
                return carry

            lax.fori_loop(0, lax.div(end - begin + 1, 2), pair, 0)
            out_ref[u] = acc[...].astype(out_ref.dtype)

    half_steps = NBLK // 2 // TSTEP

    @pl.when((step >= HSTEPS) & (step < HSTEPS + half_steps))
    def _():
        targets((step - HSTEPS) * TSTEP, sib_ref)

    @pl.when(step >= HSTEPS + half_steps)
    def _():
        targets((step - HSTEPS) * TSTEP, own_ref)


def partial_aggregates(core, order, starts, codes, pieces, half_own, half_sib, weights_t, degrees, counts):
    half_steps = NBLK // 2 // TSTEP

    def piece_at(i, meta, *_):
        return (0, lax.rem(meta[0] * (HSTEPS // 2) + jnp.minimum(i, HSTEPS - 1), HSTEPS))

    in_specs = (
        [pl.BlockSpec((PIECE, CHUNK), piece_at)] * 7
        + [
            pl.BlockSpec((PIECE, CHUNK), lambda i, *_: (0, jnp.minimum(i, HSTEPS // 2 - 1))),
            pl.BlockSpec((PIECE, CHUNK), lambda i, *_: (0, jnp.clip(i - HSTEPS // 2, 0, HSTEPS // 2 - 1))),
            pl.BlockSpec((NREL, WIDTH, WIDTH), lambda i, *_: (0, 0, 0), pipeline_mode=pl.Buffered(1)),
            pl.BlockSpec(degrees.shape, lambda i, *_: (0, 0, 0), pipeline_mode=pl.Buffered(1)),
            pl.BlockSpec(memory_space=pl.ANY),
        ]
    )
    out_specs = [
        pl.BlockSpec((TSTEP, WIDTH, BLOCK), lambda i, *_: (jnp.clip(i - HSTEPS, 0, half_steps - 1), 0, 0)),
        pl.BlockSpec((TSTEP, WIDTH, BLOCK), lambda i, *_: (jnp.clip(i - HSTEPS - half_steps, 0, half_steps - 1), 0, 0)),
    ]
    return pl.pallas_call(
        main_kernel,
        grid_spec=pltpu.PrefetchScalarGridSpec(
            num_scalar_prefetch=4,
            grid=(HSTEPS + 2 * half_steps,),
            in_specs=in_specs,
            out_specs=out_specs,
            scratch_shapes=[
                pltpu.VMEM((NREL, NBLK, WIDTH, BLOCK), jnp.bfloat16),
                pltpu.VMEM((SLOTS, BLOCK, BLOCK), jnp.int32),
                pltpu.VMEM((BLOCK, BLOCK), jnp.float32),
                pltpu.VMEM((WIDTH, BLOCK), jnp.float32),
                pltpu.SemaphoreType.DMA(()),
            ],
        ),
        out_shape=[
            jax.ShapeDtypeStruct((NBLK // 2, WIDTH, BLOCK), jnp.bfloat16),
            jax.ShapeDtypeStruct((NBLK // 2, WIDTH, BLOCK), jnp.float32),
        ],
        compiler_params=pltpu.CompilerParams(vmem_limit_bytes=52 * 1024 * 1024),
        cost_estimate=pl.CostEstimate(flops=11 * 10**9, bytes_accessed=20 * 2**20, transcendentals=0),
        name="aggregate",
    )(core, order, starts, codes, *pieces, half_own, half_sib, weights_t, degrees, counts)


def finish_kernel(parts_ref, x_ref, w_ref, bias_ref, out_ref):
    self_part = lax.dot_general(x_ref[...], w_ref[...], (((0,), (0,)), ((), ())), preferred_element_type=jnp.float32)
    for b in range(2):
        total = parts_ref[0, b].astype(jnp.float32)
        for k in range(1, parts_ref.shape[0]):
            total = total + parts_ref[k, b].astype(jnp.float32)
        rows = slice(b * BLOCK, (b + 1) * BLOCK)
        out_ref[rows, :] = jnp.maximum(total.T + self_part[rows] + bias_ref[...], 0.0).astype(jnp.bfloat16)


def finish(parts, x_own, self_weight, bias):
    return pl.pallas_call(
        finish_kernel,
        out_shape=jax.ShapeDtypeStruct((2 * BLOCK, WIDTH), jnp.bfloat16),
        compiler_params=pltpu.CompilerParams(vmem_limit_bytes=32 * 1024 * 1024),
        name="finish",
    )(parts, x_own, self_weight, bias.reshape(1, WIDTH))


def on_device(features, rel_weight, self_weight, bias, block_code, block_counts):
    row, col, core = lax.axis_index("rows"), lax.axis_index("cols"), lax.axis_index("rel")
    codes = block_code[0, 0, 0]
    counts = block_counts[0, 0, 0]

    xt = features.T
    pair_axes = ("rows", "rel")

    def fetch(array, offs):
        moves = [(r * 2 + c, shifted(r, offs[c], 1) * 2 + c) for r in range(8) for c in range(2)]
        return lax.ppermute(array, pair_axes, moves)

    def swap(array):
        return lax.ppermute(array, "rel", [(0, 1), (1, 0)])

    xt_half = lax.dynamic_slice(xt, (0, core * (NODES // 2)), (PIECE, NODES // 2))
    got = [fetch(xt, (a, b)) for a, b in zip(*OFF_CORE)]
    half_own = fetch(xt_half, (OFF_BOTH, OFF_BOTH))
    other = [swap(p) for p in got]
    half_sib = swap(half_own)
    pieces = [xt] + got + other

    order_k = piece_order(row, core)
    weights_t = rel_weight.reshape(NREL, 8, PIECE, WIDTH)[:, order_k].reshape(NREL, WIDTH, WIDTH).transpose(0, 2, 1)

    at = (row * 2 + core) * (2 * BLOCK)
    half_at = at % (NODES // 2)
    tail = jnp.where(
        (at >= NODES // 2) == (core == 1),
        lax.dynamic_slice(half_own, (0, half_at), (PIECE, 2 * BLOCK)),
        lax.dynamic_slice(half_sib, (0, half_at), (PIECE, 2 * BLOCK)),
    )
    x_rows = jnp.concatenate([lax.dynamic_slice(p, (0, at), (PIECE, 2 * BLOCK)) for p in pieces] + [tail], axis=0)
    x_own = lax.ppermute(x_rows, ("rows", "cols"), [(a * 8 + b, b * 8 + a) for a in range(8) for b in range(8)])
    self_w = self_weight.reshape(8, PIECE, WIDTH)[piece_order(col, core)].reshape(WIDTH, WIDTH)

    segment = codes // NBLK
    deg_part = partial_degrees(segment, counts)
    degrees = lax.all_to_all(jnp.broadcast_to(deg_part[None], (8,) + deg_part.shape), "cols", 0, 0)

    target = segment % NBLK
    place = jnp.where(target // 2 % 2 == core, NBLK // 2, 0) + target // 4 * 2 + target % 2
    slots = jnp.arange(SLOTS, dtype=jnp.int32)
    key = place * SLOTS + slots
    rank = jnp.sum((key[None, :] < key[:, None]).astype(jnp.int32), axis=1)
    order = jnp.sum(jnp.where(rank[None, :] == slots[:, None], slots[None, :], 0), axis=1)
    bounds = jnp.arange(NBLK + 1, dtype=jnp.int32)
    starts = jnp.sum((place[None, :] < bounds[:, None]).astype(jnp.int32), axis=1)

    to_sib, own = partial_aggregates(
        core.reshape(1).astype(jnp.int32), order, starts, codes, pieces, half_own, half_sib, weights_t, degrees, counts
    )
    both = (own + swap(to_sib).astype(jnp.float32)).astype(jnp.bfloat16)
    parts = lax.all_to_all(both.reshape(8, 2, WIDTH, BLOCK), "cols", 0, 0)
    return finish(parts, x_own, self_w, bias)


def solution(mesh):
    in_specs = (
        P("cols", "rows"),
        P("rel", None, None),
        P(),
        P(),
        P("rows", "cols", "rel", None),
        P("rows", "cols", "rel", None, None, None),
    )
    out_specs = P(("rows", "cols", "rel"), None)
    return jax.shard_map(on_device, mesh=mesh, in_specs=in_specs, out_specs=out_specs, check_vma=False)
```

```python
import jax
import jax.numpy as jnp
from jax import lax
from jax.experimental import pallas as pl
from jax.experimental.pallas import tpu as pltpu
from jax.sharding import PartitionSpec as P

BLOCK = 128
WIDTH = 512
NBLK = 32
NREL = 4
SLOTS = 128
PIECE = 64
NODES = NBLK * BLOCK
HALF = NODES // 2
CHUNK = 512
UNROLL = 4
PAIRS = 72
MIB = 1024 * 1024
NT = (((1,), (1,)), ((), ()))
TN = (((0,), (0,)), ((), ()))
VMEM_SPEC = pl.BlockSpec(memory_space=pltpu.VMEM)
SMEM_SPEC = pl.BlockSpec(memory_space=pltpu.SMEM)


def params(mib):
    return pltpu.CompilerParams(vmem_limit_bytes=mib * MIB)


def prep_kernel(codes_ref, counts_ref, weight_ref, deg_ref, cnt_ref, wt_ref):
    step = pl.program_id(0)

    @pl.when(step == 0)
    def _():
        deg_ref[...] = jnp.zeros_like(deg_ref)

    per = counts_ref.shape[0]
    ones = jnp.ones((8, BLOCK), jnp.bfloat16)
    for s in range(per):
        slot = step * per + s
        c = counts_ref[s].astype(jnp.float32).astype(jnp.bfloat16)
        cnt_ref[slot] = c
        row = lax.dot_general(ones, c, NT, preferred_element_type=jnp.float32)
        seg = lax.shift_right_logical(codes_ref[slot], 5)
        deg_ref[0, pl.ds(seg, 1), :] += row[0:1]
    wt_ref[step // 2, pl.ds(pl.multiple_of(step % 2 * 256, 256), 256), :] = weight_ref[0].T

    @pl.when(step == pl.num_programs(0) - 1)
    def _():
        for k in range(1, deg_ref.shape[0]):
            deg_ref[k] = deg_ref[0]


def prep(codes, counts, rel_weight):
    per = 16
    return pl.pallas_call(
        prep_kernel,
        grid=(SLOTS // per,),
        in_specs=[
            SMEM_SPEC,
            pl.BlockSpec((per, BLOCK, BLOCK), lambda i: (i, 0, 0)),
            pl.BlockSpec((1, WIDTH, 256), lambda i: (i // 2, 0, i % 2)),
        ],
        out_specs=[VMEM_SPEC, VMEM_SPEC, VMEM_SPEC],
        out_shape=[
            jax.ShapeDtypeStruct((8, NREL * NBLK, BLOCK), jnp.float32),
            pltpu.VMEM((SLOTS, BLOCK, BLOCK), jnp.bfloat16),
            pltpu.VMEM((NREL, WIDTH, WIDTH), jnp.bfloat16),
        ],
        compiler_params=params(24),
        cost_estimate=pl.CostEstimate(flops=2 * SLOTS * BLOCK * BLOCK * 8, bytes_accessed=10 * MIB, transcendentals=0),
        name="prep",
    )(codes, counts, rel_weight)


def scale_kernel(codes_ref, deg_ref, cnt_ref, out_ref, inv_ref):
    degree = deg_ref[0]
    for k in range(1, deg_ref.shape[0]):
        degree = degree + deg_ref[k]
    inv_ref[...] = (1.0 / jnp.maximum(degree, 1.0)).T
    out_ref[SLOTS:] = jnp.zeros_like(out_ref[SLOTS:])

    def some(q, carry):
        for u in range(8):
            slot = q * 8 + u
            seg = lax.shift_right_logical(codes_ref[slot], 5)
            scale = jnp.take_along_axis(inv_ref[...], jnp.full((BLOCK, BLOCK), seg, jnp.int32), axis=1)
            out_ref[slot] = (cnt_ref[slot].astype(jnp.float32) * scale).astype(jnp.bfloat16)
        return carry

    lax.fori_loop(0, SLOTS // 8, some, 0)


def scaled(codes, degrees, cnt):
    return pl.pallas_call(
        scale_kernel,
        in_specs=[SMEM_SPEC, VMEM_SPEC, VMEM_SPEC],
        out_specs=VMEM_SPEC,
        out_shape=pltpu.VMEM((SLOTS + 1, BLOCK, BLOCK), jnp.bfloat16),
        scratch_shapes=[pltpu.VMEM((BLOCK, BLOCK), jnp.float32)],
        compiler_params=params(24),
        cost_estimate=pl.CostEstimate(flops=4 * SLOTS * BLOCK * BLOCK, bytes_accessed=8 * MIB, transcendentals=0),
        name="scale",
    )(codes, degrees, cnt)


def hidden_chunk(half, step, x, wt_ref, hid_ref):
    per = CHUNK // BLOCK
    first = half * (NBLK // 2) + step * per

    def one(r, carry):
        h = jnp.dot(wt_ref[r], x, preferred_element_type=jnp.float32).astype(jnp.bfloat16)
        for b in range(per):
            hid_ref[r * NBLK + first + b] = h[:, b * BLOCK : (b + 1) * BLOCK]
        return carry

    lax.fori_loop(0, NREL, one, 0)


def own_hidden_kernel(core_ref, x_ref, wt_ref, hid_ref):
    hidden_chunk(core_ref[0], pl.program_id(0), x_ref[...], wt_ref, hid_ref)


HID = (NREL * NBLK, WIDTH, BLOCK)
HSTEPS = HALF // CHUNK


def own_hidden(core, x, wt):
    return pl.pallas_call(
        own_hidden_kernel,
        grid=(HSTEPS,),
        in_specs=[SMEM_SPEC, pl.BlockSpec((WIDTH, CHUNK), lambda i: (0, i)), VMEM_SPEC],
        out_specs=VMEM_SPEC,
        out_shape=pltpu.VMEM(HID, jnp.bfloat16),
        compiler_params=params(12),
        cost_estimate=pl.CostEstimate(flops=2 * HALF * WIDTH * WIDTH * NREL, bytes_accessed=4 * MIB, transcendentals=0),
        name="own_hidden",
    )(core, x, wt)


def slot_pairs(codes_ref, pairs_ref, which, hid_ref, w_ref, acc_ref):
    def some(q, carry):
        for u in range(UNROLL):
            k = q * UNROLL + u
            s1, s2, place = pairs_ref[which, 0, k], pairs_ref[which, 1, k], pairs_ref[which, 2, k]
            hs = []
            for s in (s1, s2):
                code = codes_ref[s]
                hs.append(hid_ref[lax.shift_right_logical(code, 10) * NBLK + jnp.bitwise_and(code, NBLK - 1)])
            h = jnp.concatenate(hs, axis=1)
            w = jnp.concatenate([w_ref[s1], w_ref[s2]], axis=1)
            acc_ref[place] += lax.dot_general(h, w, NT, preferred_element_type=jnp.float32)
        return carry

    lax.fori_loop(0, pairs_ref[which, 3, 0], some, 0)


def sib_kernel(core_ref, codes_ref, pairs_ref, x_ref, wt_ref, w_ref, hid_in, hid_ref, out_ref, acc):
    step = pl.program_id(0)
    hidden_chunk(1 - core_ref[0], step, x_ref[...], wt_ref, hid_ref)
    per = NBLK // 2 // HSTEPS
    acc[pl.ds(step * per, per)] = jnp.zeros((per, WIDTH, BLOCK), jnp.float32)

    @pl.when(step == HSTEPS - 1)
    def _():
        slot_pairs(codes_ref, pairs_ref, 0, hid_ref, w_ref, acc)

        def one(t, carry):
            out_ref[t] = acc[t].astype(jnp.bfloat16)
            return carry

        lax.fori_loop(0, NBLK // 2, one, 0)


def sibling_part(core, codes, pairs, x, wt, w, hid):
    return pl.pallas_call(
        sib_kernel,
        grid=(HSTEPS,),
        in_specs=[
            SMEM_SPEC, SMEM_SPEC, SMEM_SPEC,
            pl.BlockSpec((WIDTH, CHUNK), lambda i: (0, i)), VMEM_SPEC, VMEM_SPEC, VMEM_SPEC,
        ],
        out_specs=[VMEM_SPEC, VMEM_SPEC],
        out_shape=[
            pltpu.VMEM(HID, jnp.bfloat16),
            jax.ShapeDtypeStruct((NBLK // 2, WIDTH, BLOCK), jnp.bfloat16),
        ],
        input_output_aliases={6: 0},
        scratch_shapes=[pltpu.VMEM((NBLK // 2, WIDTH, BLOCK), jnp.float32)],
        compiler_params=params(16),
        cost_estimate=pl.CostEstimate(flops=2 * HALF * WIDTH * WIDTH * NREL * 2, bytes_accessed=4 * MIB, transcendentals=0),
        name="sibling_part",
    )(core, codes, pairs, x, wt, w, hid)


def own_kernel(codes_ref, pairs_ref, w_ref, hid_ref, acc):
    def one(t, carry):
        acc[t] = jnp.zeros((WIDTH, BLOCK), jnp.float32)
        return carry

    lax.fori_loop(0, NBLK // 2, one, 0)
    slot_pairs(codes_ref, pairs_ref, 1, hid_ref, w_ref, acc)


def own_part(codes, pairs, w, hid):
    return pl.pallas_call(
        own_kernel,
        in_specs=[SMEM_SPEC, SMEM_SPEC, VMEM_SPEC, VMEM_SPEC],
        out_specs=VMEM_SPEC,
        out_shape=pltpu.VMEM((NBLK // 2, WIDTH, BLOCK), jnp.float32),
        compiler_params=params(12),
        cost_estimate=pl.CostEstimate(flops=2 * HALF * WIDTH * WIDTH * NREL, bytes_accessed=4 * MIB, transcendentals=0),
        name="own_part",
    )(codes, pairs, w, hid)


def join_kernel(own_ref, other_ref, out_ref):
    out_ref[...] = (own_ref[...] + other_ref[...].astype(jnp.float32)).astype(jnp.bfloat16)


def join(own, other):
    spec = pl.BlockSpec((4, WIDTH, BLOCK), lambda i: (i, 0, 0))
    return pl.pallas_call(
        join_kernel,
        grid=(NBLK // 2 // 4,),
        in_specs=[spec, spec],
        out_specs=spec,
        out_shape=jax.ShapeDtypeStruct((NBLK // 2, WIDTH, BLOCK), jnp.bfloat16),
        compiler_params=params(12),
        cost_estimate=pl.CostEstimate(flops=MIB, bytes_accessed=8 * MIB, transcendentals=0),
        name="join",
    )(own, other)


def finish_kernel(parts_ref, x_ref, w_ref, bias_ref, out_ref):
    self_part = lax.dot_general(x_ref[...], w_ref[...], TN, preferred_element_type=jnp.float32)
    for b in range(2):
        total = parts_ref[0, b].astype(jnp.float32)
        for k in range(1, parts_ref.shape[0]):
            total = total + parts_ref[k, b].astype(jnp.float32)
        rows = slice(b * BLOCK, (b + 1) * BLOCK)
        out_ref[rows, :] = jnp.maximum(total.T + self_part[rows] + bias_ref[...], 0.0).astype(jnp.bfloat16)


def finish(parts, x_own, self_weight, bias):
    return pl.pallas_call(
        finish_kernel,
        out_shape=jax.ShapeDtypeStruct((2 * BLOCK, WIDTH), jnp.bfloat16),
        compiler_params=params(32),
        name="finish",
    )(parts, x_own, self_weight, bias.reshape(1, WIDTH))


def pair_lists(codes, core):
    slots = jnp.arange(SLOTS, dtype=jnp.int32)
    target = codes // NBLK % NBLK
    half = (target // 2 % 2 == core).astype(jnp.int32)
    place = target // 4 * 2 + target % 2
    group = half * (NBLK // 2) + place
    same = group[None, :] == group[:, None]
    nth = jnp.sum((same & (slots[None, :] < slots[:, None])).astype(jnp.int32), axis=1)
    groups = jnp.arange(NBLK, dtype=jnp.int32)
    size = jnp.sum((group[None, :] == groups[:, None]).astype(jnp.int32), axis=1)
    need = (size + 1) // 2
    before = (groups[None, :] < groups[:, None]) & (groups[None, :] // (NBLK // 2) == groups[:, None] // (NBLK // 2))
    base = jnp.sum(jnp.where(before, need[None, :], 0), axis=1)
    at = half * PAIRS + nth // 2 + jnp.sum(jnp.where(group[:, None] == groups[None, :], base[None, :], 0), axis=1)
    entries = jnp.arange(2 * PAIRS, dtype=jnp.int32)
    match = at[None, :] == entries[:, None]
    is_first = match & (nth % 2 == 0)[None, :]
    is_second = match & (nth % 2 == 1)[None, :]
    first = SLOTS + jnp.sum(jnp.where(is_first, slots[None, :] - SLOTS, 0), axis=1)
    second = SLOTS + jnp.sum(jnp.where(is_second, slots[None, :] - SLOTS, 0), axis=1)
    where = jnp.sum(jnp.where(is_first, place[None, :], 0), axis=1)
    steps = (jnp.sum(need.reshape(2, NBLK // 2), axis=1) + UNROLL - 1) // UNROLL
    steps = jnp.broadcast_to(steps[:, None], (2, PAIRS))
    return jnp.stack([first.reshape(2, PAIRS), second.reshape(2, PAIRS), where.reshape(2, PAIRS), steps], axis=1)


def swap(array):
    return lax.ppermute(array, "rel", [(0, 1), (1, 0)])


def on_device(features, rel_weight, self_weight, bias, block_code, block_counts):
    row, core = lax.axis_index("rows"), lax.axis_index("rel")
    codes = block_code[0, 0, 0]
    counts = block_counts[0, 0, 0]
    core_arg = core.reshape(1).astype(jnp.int32)
    padded = jnp.concatenate([codes, jnp.zeros((8,), jnp.int32)])

    x_half = lax.dynamic_slice(features.T, (0, core * HALF), (PIECE, HALF))
    x_mine = lax.all_to_all(jnp.broadcast_to(x_half[None], (8, PIECE, HALF)), "rows", 0, 0)
    x_mine = x_mine.reshape(WIDTH, HALF)

    deg_parts, cnt, wt = prep(codes, counts, rel_weight)
    degrees = lax.all_to_all(deg_parts, "cols", 0, 0)
    w = scaled(codes, degrees, cnt)
    pairs = pair_lists(codes, core)

    x_other = swap(x_mine)
    x_rows = lax.dynamic_slice(x_mine, (0, row * (2 * BLOCK)), (WIDTH, 2 * BLOCK))
    moves = [
        ((a * 8 + b) * 2 + g, (b * 8 + 4 * g + a // 2) * 2 + a % 2) for a in range(8) for b in range(8) for g in range(2)
    ]
    x_own = lax.ppermute(x_rows, ("rows", "cols", "rel"), moves)

    hid = own_hidden(core_arg, x_mine, wt)
    hid, to_sib = sibling_part(core_arg, padded, pairs, x_other, wt, w, hid)
    other = swap(to_sib)
    own = own_part(padded, pairs, w, hid)
    both = join(own, other)
    both, x_own = lax.optimization_barrier((both, x_own))
    parts = lax.all_to_all(both.reshape(8, 2, WIDTH, BLOCK), "cols", 0, 0)
    return finish(parts, x_own, self_weight, bias)


def solution(mesh):
    in_specs = (
        P("cols", "rows"),
        P("rel", None, None),
        P(),
        P(),
        P("rows", "cols", "rel", None),
        P("rows", "cols", "rel", None, None, None),
    )
    out_specs = P(("rows", "cols", "rel"), None)
    return jax.shard_map(on_device, mesh=mesh, in_specs=in_specs, out_specs=out_specs, check_vma=False)
```

```python
import jax
import jax.numpy as jnp
from jax import lax
from jax.experimental import pallas as pl
from jax.experimental.pallas import tpu as pltpu
from jax.sharding import PartitionSpec as P

BLOCK = 128
WIDTH = 512
NBLK = 32
NREL = 4
SLOTS = 128
PIECE = 64
NODES = NBLK * BLOCK
HALF = NODES // 2
CHUNK = 512
UNROLL = 8
PAIRS = 72
MIB = 1024 * 1024
NT = (((1,), (1,)), ((), ()))
TN = (((0,), (0,)), ((), ()))
VMEM_SPEC = pl.BlockSpec(memory_space=pltpu.VMEM)
SMEM_SPEC = pl.BlockSpec(memory_space=pltpu.SMEM)


def params(mib):
    return pltpu.CompilerParams(vmem_limit_bytes=mib * MIB)


def prep_kernel(codes_ref, counts_ref, weight_ref, deg_ref, wt_ref):
    step = pl.program_id(0)

    @pl.when(step == 0)
    def _():
        deg_ref[...] = jnp.zeros_like(deg_ref)

    per = counts_ref.shape[0]
    ones = jnp.ones((8, BLOCK), jnp.bfloat16)
    for s in range(per):
        c = counts_ref[s].astype(jnp.float32).astype(jnp.bfloat16)
        row = lax.dot_general(ones, c, NT, preferred_element_type=jnp.float32)
        seg = lax.shift_right_logical(codes_ref[step * per + s], 5)
        deg_ref[pl.ds(seg, 1), :] += row[0:1]
    wt_ref[0] = weight_ref[0].T


def prep(codes, counts, rel_weight):
    per = 16
    return pl.pallas_call(
        prep_kernel,
        grid=(SLOTS // per,),
        in_specs=[
            SMEM_SPEC,
            pl.BlockSpec((per, BLOCK, BLOCK), lambda i: (i, 0, 0)),
            pl.BlockSpec((1, WIDTH, 256), lambda i: (i // 2, 0, i % 2)),
        ],
        out_specs=[
            pl.BlockSpec((NREL * NBLK, BLOCK), lambda i: (0, 0)),
            pl.BlockSpec((1, 256, WIDTH), lambda i: (i // 2, i % 2, 0)),
        ],
        out_shape=[
            jax.ShapeDtypeStruct((NREL * NBLK, BLOCK), jnp.float32),
            jax.ShapeDtypeStruct((NREL, WIDTH, WIDTH), jnp.bfloat16),
        ],
        compiler_params=params(58),
        cost_estimate=pl.CostEstimate(flops=2 * SLOTS * BLOCK * BLOCK * 8, bytes_accessed=12 * MIB, transcendentals=0),
        name="prep",
    )(codes, counts, rel_weight)


def scale_kernel(codes_ref, *refs):
    deg_refs, (counts_ref, out_ref, inv_ref) = refs[:8], refs[8:]
    step = pl.program_id(0)

    @pl.when(step == 0)
    def _():
        degree = deg_refs[0][...]
        for ref in deg_refs[1:]:
            degree = degree + ref[...]
        inv_ref[...] = (1.0 / jnp.maximum(degree, 1.0)).T

    per = counts_ref.shape[0]
    for u in range(per):
        slot = step * per + u
        seg = lax.shift_right_logical(codes_ref[slot], 5)
        scale = jnp.take_along_axis(inv_ref[...], jnp.full((BLOCK, BLOCK), seg, jnp.int32), axis=1)
        out_ref[u] = (counts_ref[u].astype(jnp.float32) * scale).astype(jnp.bfloat16)


def scaled(codes, degrees, counts):
    per = 16
    return pl.pallas_call(
        scale_kernel,
        grid=(SLOTS // per,),
        in_specs=[SMEM_SPEC]
        + [pl.BlockSpec((NREL * NBLK, BLOCK), lambda i: (0, 0))] * 8
        + [pl.BlockSpec((per, BLOCK, BLOCK), lambda i: (i, 0, 0))],
        out_specs=pl.BlockSpec((per, BLOCK, BLOCK), lambda i: (i, 0, 0)),
        out_shape=jax.ShapeDtypeStruct((SLOTS, BLOCK, BLOCK), jnp.bfloat16),
        scratch_shapes=[pltpu.VMEM((BLOCK, BLOCK), jnp.float32)],
        compiler_params=params(58),
        cost_estimate=pl.CostEstimate(flops=4 * SLOTS * BLOCK * BLOCK, bytes_accessed=13 * MIB, transcendentals=0),
        name="scale",
    )(codes, *degrees, counts)


HID = (NREL * NBLK, WIDTH, BLOCK)


def hidden_half(half, x_ref, wt_ref, hid_ref, ready):
    per = CHUNK // BLOCK

    def one(r, carry):
        ready(r)
        for n in range(HALF // CHUNK):
            x = x_ref[:, n * CHUNK : (n + 1) * CHUNK]
            h = jnp.dot(wt_ref[r], x, preferred_element_type=jnp.float32).astype(jnp.bfloat16)
            for b in range(per):
                hid_ref[r * NBLK + half * (NBLK // 2) + n * per + b] = h[:, b * BLOCK : (b + 1) * BLOCK]
        return carry

    lax.fori_loop(0, NREL, one, 0)


def own_hidden_kernel(place_ref, x_ref, wt_hbm, w_hbm, hid_ref, wt_ref, w_ref, rows_ref, sems):
    copies = [pltpu.make_async_copy(wt_hbm.at[r], wt_ref.at[r], sems.at[r]) for r in range(NREL)]
    copies.append(pltpu.make_async_copy(w_hbm, w_ref.at[pl.ds(0, SLOTS)], sems.at[NREL]))
    for copy in copies:
        copy.start()
    w_ref[SLOTS] = jnp.zeros((BLOCK, BLOCK), jnp.bfloat16)
    at = pl.multiple_of(place_ref[1] * (2 * BLOCK), 2 * BLOCK)
    rows_ref[...] = x_ref[:, pl.ds(at, 2 * BLOCK)]

    def ready(r):
        pltpu.make_async_copy(wt_hbm.at[r], wt_ref.at[r], sems.at[r]).wait()

    hidden_half(place_ref[0], x_ref, wt_ref, hid_ref, ready)
    copies[-1].wait()


def own_hidden(place, x, wt, w):
    return pl.pallas_call(
        own_hidden_kernel,
        in_specs=[SMEM_SPEC, VMEM_SPEC, pl.BlockSpec(memory_space=pl.ANY), pl.BlockSpec(memory_space=pl.ANY)],
        out_specs=[VMEM_SPEC] * 4,
        out_shape=[
            pltpu.VMEM(HID, jnp.bfloat16),
            pltpu.VMEM((NREL, WIDTH, WIDTH), jnp.bfloat16),
            pltpu.VMEM((SLOTS + 1, BLOCK, BLOCK), jnp.bfloat16),
            jax.ShapeDtypeStruct((WIDTH, 2 * BLOCK), jnp.bfloat16),
        ],
        scratch_shapes=[pltpu.SemaphoreType.DMA((NREL + 1,))],
        compiler_params=params(12),
        cost_estimate=pl.CostEstimate(flops=2 * HALF * WIDTH * WIDTH * NREL, bytes_accessed=8 * MIB, transcendentals=0),
        name="own_hidden",
    )(place, x, wt, w)


def slot_pairs(codes_ref, pairs_ref, which, hid_ref, w_ref, acc_ref):
    def some(q, carry):
        for u in range(UNROLL):
            k = q * UNROLL + u
            s1, s2, place = pairs_ref[which, 0, k], pairs_ref[which, 1, k], pairs_ref[which, 2, k]
            hs = []
            for s in (s1, s2):
                code = codes_ref[s]
                hs.append(hid_ref[lax.shift_right_logical(code, 10) * NBLK + jnp.bitwise_and(code, NBLK - 1)])
            h = jnp.concatenate(hs, axis=1)
            w = jnp.concatenate([w_ref[s1], w_ref[s2]], axis=1)
            acc_ref[place] += lax.dot_general(h, w, NT, preferred_element_type=jnp.float32)
        return carry

    lax.fori_loop(0, pairs_ref[which, 3, 0], some, 0)


def clear(acc):
    def one(t, carry):
        acc[t] = jnp.zeros((WIDTH, BLOCK), jnp.float32)
        return carry

    lax.fori_loop(0, NBLK // 2, one, 0)


def sib_kernel(place_ref, codes_ref, pairs_ref, x_ref, wt_ref, w_ref, hid_in, hid_ref, out_ref, acc):
    hidden_half(1 - place_ref[0], x_ref, wt_ref, hid_ref, lambda r: None)
    clear(acc)
    slot_pairs(codes_ref, pairs_ref, 0, hid_ref, w_ref, acc)

    def one(t, carry):
        out_ref[t] = acc[t].astype(jnp.bfloat16)
        return carry

    lax.fori_loop(0, NBLK // 2, one, 0)


def sibling_part(place, codes, pairs, x, wt, w, hid):
    return pl.pallas_call(
        sib_kernel,
        in_specs=[SMEM_SPEC] * 3 + [VMEM_SPEC] * 4,
        out_specs=[VMEM_SPEC, VMEM_SPEC],
        out_shape=[
            pltpu.VMEM(HID, jnp.bfloat16),
            pltpu.VMEM((NBLK // 2, WIDTH, BLOCK), jnp.bfloat16),
        ],
        input_output_aliases={6: 0},
        scratch_shapes=[pltpu.VMEM((NBLK // 2, WIDTH, BLOCK), jnp.float32)],
        compiler_params=params(16),
        cost_estimate=pl.CostEstimate(flops=2 * HALF * WIDTH * WIDTH * NREL * 2, bytes_accessed=4 * MIB, transcendentals=0),
        name="sibling_part",
    )(place, codes, pairs, x, wt, w, hid)


def own_kernel(codes_ref, pairs_ref, w_ref, hid_ref, acc):
    clear(acc)
    slot_pairs(codes_ref, pairs_ref, 1, hid_ref, w_ref, acc)


def own_part(codes, pairs, w, hid):
    return pl.pallas_call(
        own_kernel,
        in_specs=[SMEM_SPEC, SMEM_SPEC, VMEM_SPEC, VMEM_SPEC],
        out_specs=VMEM_SPEC,
        out_shape=pltpu.VMEM((NBLK // 2, WIDTH, BLOCK), jnp.float32),
        compiler_params=params(12),
        cost_estimate=pl.CostEstimate(flops=2 * HALF * WIDTH * WIDTH * NREL, bytes_accessed=4 * MIB, transcendentals=0),
        name="own_part",
    )(codes, pairs, w, hid)


def join_kernel(own_ref, other_ref, out_ref):
    per = out_ref.shape[0]
    step = pl.program_id(0)
    for t in range(per):
        out_ref[t] = (own_ref[step * per + t] + other_ref[t].astype(jnp.float32)).astype(jnp.bfloat16)


def join(own, other):
    spec = pl.BlockSpec((4, WIDTH, BLOCK), lambda i: (i, 0, 0))
    return pl.pallas_call(
        join_kernel,
        grid=(NBLK // 2 // 4,),
        in_specs=[VMEM_SPEC, spec],
        out_specs=spec,
        out_shape=jax.ShapeDtypeStruct((NBLK // 2, WIDTH, BLOCK), jnp.bfloat16),
        compiler_params=params(12),
        cost_estimate=pl.CostEstimate(flops=MIB, bytes_accessed=8 * MIB, transcendentals=0),
        name="join",
    )(own, other)


def finish_kernel(parts_ref, x_ref, w_ref, bias_ref, out_ref):
    self_part = lax.dot_general(x_ref[...], w_ref[...], TN, preferred_element_type=jnp.float32)
    for b in range(2):
        total = parts_ref[0, b].astype(jnp.float32)
        for k in range(1, parts_ref.shape[0]):
            total = total + parts_ref[k, b].astype(jnp.float32)
        rows = slice(b * BLOCK, (b + 1) * BLOCK)
        out_ref[rows, :] = jnp.maximum(total.T + self_part[rows] + bias_ref[...], 0.0).astype(jnp.bfloat16)


def finish(parts, x_own, self_weight, bias):
    return pl.pallas_call(
        finish_kernel,
        out_shape=jax.ShapeDtypeStruct((2 * BLOCK, WIDTH), jnp.bfloat16),
        compiler_params=params(32),
        name="finish",
    )(parts, x_own, self_weight, bias.reshape(1, WIDTH))


def pair_lists(codes, core):
    slots = jnp.arange(SLOTS, dtype=jnp.int32)
    target = codes // NBLK % NBLK
    half = (target // 2 % 2 == core).astype(jnp.int32)
    place = target // 4 * 2 + target % 2
    group = half * (NBLK // 2) + place
    same = group[None, :] == group[:, None]
    nth = jnp.sum((same & (slots[None, :] < slots[:, None])).astype(jnp.int32), axis=1)
    groups = jnp.arange(NBLK, dtype=jnp.int32)
    size = jnp.sum((group[None, :] == groups[:, None]).astype(jnp.int32), axis=1)
    need = (size + 1) // 2
    before = (groups[None, :] < groups[:, None]) & (groups[None, :] // (NBLK // 2) == groups[:, None] // (NBLK // 2))
    base = jnp.sum(jnp.where(before, need[None, :], 0), axis=1)
    at = half * PAIRS + nth // 2 + jnp.sum(jnp.where(group[:, None] == groups[None, :], base[None, :], 0), axis=1)
    entries = jnp.arange(2 * PAIRS, dtype=jnp.int32)
    match = at[None, :] == entries[:, None]
    is_first = match & (nth % 2 == 0)[None, :]
    is_second = match & (nth % 2 == 1)[None, :]
    first = SLOTS + jnp.sum(jnp.where(is_first, slots[None, :] - SLOTS, 0), axis=1)
    second = SLOTS + jnp.sum(jnp.where(is_second, slots[None, :] - SLOTS, 0), axis=1)
    where = jnp.sum(jnp.where(is_first, place[None, :], 0), axis=1)
    steps = (jnp.sum(need.reshape(2, NBLK // 2), axis=1) + UNROLL - 1) // UNROLL
    steps = jnp.broadcast_to(steps[:, None], (2, PAIRS))
    return jnp.stack([first.reshape(2, PAIRS), second.reshape(2, PAIRS), where.reshape(2, PAIRS), steps], axis=1)


def swap(array):
    return lax.ppermute(array, "rel", [(0, 1), (1, 0)])


def gather_half(x_half):
    return lax.all_to_all(jnp.broadcast_to(x_half[None], (8, PIECE, HALF)), "rows", 0, 0).reshape(WIDTH, HALF)


def on_device(features, rel_weight, self_weight, bias, block_code, block_counts):
    row, core = lax.axis_index("rows"), lax.axis_index("rel")
    codes = block_code[0, 0, 0]
    counts = block_counts[0, 0, 0]
    place = jnp.stack([core, row]).astype(jnp.int32)
    padded = jnp.concatenate([codes, jnp.zeros((8,), jnp.int32)])

    x_half = lax.dynamic_slice(features.T, (0, core * HALF), (PIECE, HALF))
    x_mine = gather_half(x_half)

    deg_part, wt = prep(codes, counts, rel_weight)
    degrees = [deg_part] + [lax.ppermute(deg_part, "cols", [(i, (i + k) % 8) for i in range(8)]) for k in range(1, 8)]
    w = scaled(codes, degrees, counts)
    pairs = pair_lists(codes, core)
    x_mine, w, pairs, padded, place = lax.optimization_barrier((x_mine, w, pairs, padded, place))

    x_other = swap(x_mine)
    hid, wt, w, x_rows = own_hidden(place, x_mine, wt, w)
    moves = [
        ((a * 8 + b) * 2 + g, (b * 8 + 4 * g + a // 2) * 2 + a % 2) for a in range(8) for b in range(8) for g in range(2)
    ]
    x_own = lax.ppermute(x_rows, ("rows", "cols", "rel"), moves)
    hid, to_sib = sibling_part(place, padded, pairs, x_other, wt, w, hid)
    other = swap(to_sib)
    own = own_part(padded, pairs, w, hid)
    both = join(own, other)
    both, x_own = lax.optimization_barrier((both, x_own))
    parts = lax.all_to_all(both.reshape(8, 2, WIDTH, BLOCK), "cols", 0, 0)
    return finish(parts, x_own, self_weight, bias)


def solution(mesh):
    in_specs = (
        P("cols", "rows"),
        P("rel", None, None),
        P(),
        P(),
        P("rows", "cols", "rel", None),
        P("rows", "cols", "rel", None, None, None),
    )
    out_specs = P(("rows", "cols", "rel"), None)
    return jax.shard_map(on_device, mesh=mesh, in_specs=in_specs, out_specs=out_specs, check_vma=False)
```

```python
import jax
import jax.numpy as jnp
from jax import lax
from jax.experimental import pallas as pl
from jax.experimental.pallas import tpu as pltpu
from jax.sharding import PartitionSpec as P

BLOCK = 128
WIDTH = 512
NBLK = 32
NREL = 4
SLOTS = 128
PIECE = 64
NODES = NBLK * BLOCK
HALF = NODES // 2
CHUNK = 512
UNROLL = 8
PAIRS = 72
MIB = 1024 * 1024
NT = (((1,), (1,)), ((), ()))
TN = (((0,), (0,)), ((), ()))
VMEM_SPEC = pl.BlockSpec(memory_space=pltpu.VMEM)
SMEM_SPEC = pl.BlockSpec(memory_space=pltpu.SMEM)


def params(mib):
    return pltpu.CompilerParams(vmem_limit_bytes=mib * MIB)


ANY_SPEC = pl.BlockSpec(memory_space=pl.ANY)
CHUNKS = 8
PER = SLOTS // CHUNKS


def counts_copies(hbm, vmem, sems):
    def copy(i):
        at = pl.ds(i * PER, PER)
        return pltpu.make_async_copy(hbm.at[at], vmem.at[at], sems.at[i])

    return copy


def prep_kernel(codes_ref, counts_hbm, weight_hbm, deg_ref, cnt_hbm, wt_hbm, counts, cnt, weight, wt, sems):
    counts_copy = counts_copies(counts_hbm, counts, sems)
    weight_copy = pltpu.make_async_copy(weight_hbm, weight, sems.at[CHUNKS])
    wt_copy = pltpu.make_async_copy(wt, wt_hbm, sems.at[CHUNKS + 1])
    weight_copy.start()
    for i in range(CHUNKS):
        counts_copy(i).start()
    deg_ref[...] = jnp.zeros_like(deg_ref)
    weight_copy.wait()

    def turn(r, carry):
        wt[r] = weight[r].T
        return carry

    lax.fori_loop(0, NREL, turn, 0)
    wt_copy.start()
    ones = jnp.ones((8, BLOCK), jnp.bfloat16)

    def cnt_copy(i):
        at = pl.ds(i * PER, PER)
        return pltpu.make_async_copy(cnt.at[at], cnt_hbm.at[at], sems.at[CHUNKS + 2 + i])

    def some(i, carry):
        counts_copy(i).wait()
        for s in range(PER):
            slot = i * PER + s
            c = counts[slot].astype(jnp.float32).astype(jnp.bfloat16)
            cnt[slot] = c
            row = lax.dot_general(ones, c, NT, preferred_element_type=jnp.float32)
            seg = lax.shift_right_logical(codes_ref[slot], 5)
            deg_ref[pl.ds(seg, 1), :] += row[0:1]
        cnt_copy(i).start()
        return carry

    lax.fori_loop(0, CHUNKS, some, 0)
    wt_copy.wait()
    for i in range(CHUNKS):
        cnt_copy(i).wait()


def prep(codes, counts, rel_weight):
    return pl.pallas_call(
        prep_kernel,
        in_specs=[SMEM_SPEC, ANY_SPEC, ANY_SPEC],
        out_specs=[VMEM_SPEC, ANY_SPEC, ANY_SPEC],
        out_shape=[
            jax.ShapeDtypeStruct((NREL * NBLK, BLOCK), jnp.float32),
            jax.ShapeDtypeStruct((SLOTS, BLOCK, BLOCK), jnp.bfloat16),
            jax.ShapeDtypeStruct((NREL, WIDTH, WIDTH), jnp.bfloat16),
        ],
        scratch_shapes=[
            pltpu.VMEM((SLOTS, BLOCK, BLOCK), jnp.int32),
            pltpu.VMEM((SLOTS, BLOCK, BLOCK), jnp.bfloat16),
            pltpu.VMEM((NREL, WIDTH, WIDTH), jnp.bfloat16),
            pltpu.VMEM((NREL, WIDTH, WIDTH), jnp.bfloat16),
            pltpu.SemaphoreType.DMA((2 * CHUNKS + 2,)),
        ],
        compiler_params=params(58),
        cost_estimate=pl.CostEstimate(flops=2 * SLOTS * BLOCK * BLOCK * 8, bytes_accessed=16 * MIB, transcendentals=0),
        name="prep",
    )(codes, counts, rel_weight)


HALF_BLOCKS = NBLK // 2
HID = (NREL, NBLK, WIDTH, BLOCK)


def hidden_half(first, x_ref, wt_ref, hid_ref, before, after):
    per = CHUNK // BLOCK

    def one(r, carry):
        before(r)
        for n in range(HALF // CHUNK):
            x = x_ref[:, n * CHUNK : (n + 1) * CHUNK]
            h = jnp.dot(wt_ref[r], x, preferred_element_type=jnp.float32).astype(jnp.bfloat16)
            for b in range(per):
                hid_ref[r, first + n * per + b] = h[:, b * BLOCK : (b + 1) * BLOCK]
        after(r)
        return carry

    lax.fori_loop(0, NREL, one, 0)


def own_hidden_kernel(x_ref, wt_hbm, hid_hbm, hid, wt, sems):
    def wt_copy(r):
        return pltpu.make_async_copy(wt_hbm.at[r], wt.at[r], sems.at[r])

    def hid_copy(r):
        return pltpu.make_async_copy(hid.at[r], hid_hbm.at[r], sems.at[NREL + r])

    for r in range(NREL):
        wt_copy(r).start()
    hidden_half(0, x_ref, wt, hid, lambda r: wt_copy(r).wait(), lambda r: hid_copy(r).start())
    for r in range(NREL):
        hid_copy(r).wait()


def own_hidden(x, wt):
    shape = (NREL, HALF_BLOCKS, WIDTH, BLOCK)
    return pl.pallas_call(
        own_hidden_kernel,
        in_specs=[VMEM_SPEC, ANY_SPEC],
        out_specs=ANY_SPEC,
        out_shape=jax.ShapeDtypeStruct(shape, jnp.bfloat16),
        scratch_shapes=[
            pltpu.VMEM(shape, jnp.bfloat16),
            pltpu.VMEM((NREL, WIDTH, WIDTH), jnp.bfloat16),
            pltpu.SemaphoreType.DMA((2 * NREL,)),
        ],
        compiler_params=params(56),
        cost_estimate=pl.CostEstimate(flops=2 * HALF * WIDTH * WIDTH * NREL, bytes_accessed=12 * MIB, transcendentals=0),
        name="own_hidden",
    )(x, wt)


def slot_pairs(codes_ref, pairs_ref, which, hid_ref, w_ref, acc_ref):
    def some(q, carry):
        for u in range(UNROLL):
            k = q * UNROLL + u
            s1, s2, place = pairs_ref[which, 0, k], pairs_ref[which, 1, k], pairs_ref[which, 2, k]
            hs = []
            for s in (s1, s2):
                code = codes_ref[s]
                hs.append(hid_ref[lax.shift_right_logical(code, 10), jnp.bitwise_and(code, NBLK - 1)])
            h = jnp.concatenate(hs, axis=1)
            w = jnp.concatenate([w_ref[s1], w_ref[s2]], axis=1)
            acc_ref[place] += lax.dot_general(h, w, NT, preferred_element_type=jnp.float32)
        return carry

    lax.fori_loop(0, pairs_ref[which, 3, 0], some, 0)


def rest_kernel(place_ref, codes_ref, pairs_ref, *refs):
    deg_refs, refs = refs[:8], refs[8:]
    x_ref, wt_hbm, cnt_hbm, hid_hbm, sib_hbm, own_ref, hid, wt, w, acc, sib, inv_ref, sems = refs
    core = place_ref[0]
    other_first = (1 - core) * HALF_BLOCKS

    def wt_copy(r):
        return pltpu.make_async_copy(wt_hbm.at[r], wt.at[r], sems.at[r])

    def hid_copy(r):
        return pltpu.make_async_copy(hid_hbm.at[r], hid.at[r, pl.ds(core * HALF_BLOCKS, HALF_BLOCKS)], sems.at[NREL + r])

    def cnt_copy(r):
        at = pl.ds(r * (SLOTS // NREL), SLOTS // NREL)
        return pltpu.make_async_copy(cnt_hbm.at[at], w.at[at], sems.at[2 * NREL + r])

    sib_copy = pltpu.make_async_copy(sib, sib_hbm, sems.at[3 * NREL])
    for r in range(NREL):
        wt_copy(r).start()
        cnt_copy(r).start()
    for r in range(NREL):
        hid_copy(r).start()
    degree = deg_refs[0][...]
    for ref in deg_refs[1:]:
        degree = degree + ref[...]
    inv_ref[...] = (1.0 / jnp.maximum(degree, 1.0)).T
    w[SLOTS] = jnp.zeros((BLOCK, BLOCK), jnp.bfloat16)

    def before(r):
        wt_copy(r).wait()
        cnt_copy(r).wait()
        for u in range(SLOTS // NREL):
            slot = r * (SLOTS // NREL) + u
            seg = lax.shift_right_logical(codes_ref[slot], 5)
            factor = jnp.take_along_axis(inv_ref[...], jnp.full((BLOCK, BLOCK), seg, jnp.int32), axis=1)
            w[slot] = (w[slot].astype(jnp.float32) * factor).astype(jnp.bfloat16)
        zeros = jnp.zeros((HALF_BLOCKS // NREL, WIDTH, BLOCK), jnp.float32)
        acc[pl.ds(r * (HALF_BLOCKS // NREL), HALF_BLOCKS // NREL)] = zeros
        own_ref[pl.ds(r * (HALF_BLOCKS // NREL), HALF_BLOCKS // NREL)] = zeros

    hidden_half(other_first, x_ref, wt, hid, before, lambda r: None)
    for r in range(NREL):
        hid_copy(r).wait()
    slot_pairs(codes_ref, pairs_ref, 0, hid, w, acc)

    def one(t, carry):
        sib[t] = acc[t].astype(jnp.bfloat16)
        return carry

    lax.fori_loop(0, HALF_BLOCKS, one, 0)
    sib_copy.start()
    slot_pairs(codes_ref, pairs_ref, 1, hid, w, own_ref)
    sib_copy.wait()


def rest(place, codes, pairs, degrees, x, wt, cnt, hid):
    return pl.pallas_call(
        rest_kernel,
        in_specs=[SMEM_SPEC] * 3 + [VMEM_SPEC] * 9 + [ANY_SPEC] * 3,
        out_specs=[ANY_SPEC, VMEM_SPEC],
        out_shape=[
            jax.ShapeDtypeStruct((HALF_BLOCKS, WIDTH, BLOCK), jnp.bfloat16),
            jax.ShapeDtypeStruct((HALF_BLOCKS, WIDTH, BLOCK), jnp.float32),
        ],
        scratch_shapes=[
            pltpu.VMEM(HID, jnp.bfloat16),
            pltpu.VMEM((NREL, WIDTH, WIDTH), jnp.bfloat16),
            pltpu.VMEM((SLOTS + 1, BLOCK, BLOCK), jnp.bfloat16),
            pltpu.VMEM((HALF_BLOCKS, WIDTH, BLOCK), jnp.float32),
            pltpu.VMEM((HALF_BLOCKS, WIDTH, BLOCK), jnp.bfloat16),
            pltpu.VMEM((BLOCK, BLOCK), jnp.float32),
            pltpu.SemaphoreType.DMA((3 * NREL + 1,)),
        ],
        compiler_params=params(REST_MIB),
        cost_estimate=pl.CostEstimate(flops=2 * HALF * WIDTH * WIDTH * NREL * 3, bytes_accessed=20 * MIB, transcendentals=0),
        name="rest",
    )(place, codes, pairs, *degrees, x, wt, cnt, hid)


REST_MIB = 50


def join_kernel(own_ref, other_ref, out_ref):
    per = out_ref.shape[0]
    step = pl.program_id(0)
    for t in range(per):
        out_ref[t] = (own_ref[step * per + t] + other_ref[t].astype(jnp.float32)).astype(jnp.bfloat16)


def join(own, other):
    spec = pl.BlockSpec((4, WIDTH, BLOCK), lambda i: (i, 0, 0))
    return pl.pallas_call(
        join_kernel,
        grid=(NBLK // 2 // 4,),
        in_specs=[VMEM_SPEC, spec],
        out_specs=spec,
        out_shape=jax.ShapeDtypeStruct((NBLK // 2, WIDTH, BLOCK), jnp.bfloat16),
        compiler_params=params(12),
        cost_estimate=pl.CostEstimate(flops=MIB, bytes_accessed=8 * MIB, transcendentals=0),
        name="join",
    )(own, other)


def finish_kernel(parts_ref, x_ref, w_ref, bias_ref, out_ref):
    self_part = lax.dot_general(x_ref[...], w_ref[...], TN, preferred_element_type=jnp.float32)
    for b in range(2):
        total = parts_ref[0, b].astype(jnp.float32)
        for k in range(1, parts_ref.shape[0]):
            total = total + parts_ref[k, b].astype(jnp.float32)
        rows = slice(b * BLOCK, (b + 1) * BLOCK)
        out_ref[rows, :] = jnp.maximum(total.T + self_part[rows] + bias_ref[...], 0.0).astype(jnp.bfloat16)


def finish(parts, x_own, self_weight, bias):
    return pl.pallas_call(
        finish_kernel,
        out_shape=jax.ShapeDtypeStruct((2 * BLOCK, WIDTH), jnp.bfloat16),
        compiler_params=params(32),
        name="finish",
    )(parts, x_own, self_weight, bias.reshape(1, WIDTH))


def pair_lists(codes, core):
    slots = jnp.arange(SLOTS, dtype=jnp.int32)
    target = codes // NBLK % NBLK
    half = (target // 2 % 2 == core).astype(jnp.int32)
    place = target // 4 * 2 + target % 2
    group = half * (NBLK // 2) + place
    same = group[None, :] == group[:, None]
    nth = jnp.sum((same & (slots[None, :] < slots[:, None])).astype(jnp.int32), axis=1)
    groups = jnp.arange(NBLK, dtype=jnp.int32)
    size = jnp.sum((group[None, :] == groups[:, None]).astype(jnp.int32), axis=1)
    need = (size + 1) // 2
    before = (groups[None, :] < groups[:, None]) & (groups[None, :] // (NBLK // 2) == groups[:, None] // (NBLK // 2))
    base = jnp.sum(jnp.where(before, need[None, :], 0), axis=1)
    at = half * PAIRS + nth // 2 + jnp.sum(jnp.where(group[:, None] == groups[None, :], base[None, :], 0), axis=1)
    entries = jnp.arange(2 * PAIRS, dtype=jnp.int32)
    match = at[None, :] == entries[:, None]
    is_first = match & (nth % 2 == 0)[None, :]
    is_second = match & (nth % 2 == 1)[None, :]
    first = SLOTS + jnp.sum(jnp.where(is_first, slots[None, :] - SLOTS, 0), axis=1)
    second = SLOTS + jnp.sum(jnp.where(is_second, slots[None, :] - SLOTS, 0), axis=1)
    where = jnp.sum(jnp.where(is_first, place[None, :], 0), axis=1)
    steps = (jnp.sum(need.reshape(2, NBLK // 2), axis=1) + UNROLL - 1) // UNROLL
    steps = jnp.broadcast_to(steps[:, None], (2, PAIRS))
    return jnp.stack([first.reshape(2, PAIRS), second.reshape(2, PAIRS), where.reshape(2, PAIRS), steps], axis=1)


def swap(array):
    return lax.ppermute(array, "rel", [(0, 1), (1, 0)])


def on_device(features, rel_weight, self_weight, bias, block_code, block_counts):
    row, col, core = lax.axis_index("rows"), lax.axis_index("cols"), lax.axis_index("rel")
    codes = block_code[0, 0, 0]
    counts = block_counts[0, 0, 0]
    place = jnp.stack([core, row]).astype(jnp.int32)
    padded = jnp.concatenate([codes, jnp.zeros((8,), jnp.int32)])

    x_half = lax.dynamic_slice(features.T, (0, core * HALF), (PIECE, HALF))
    x_sent = jnp.broadcast_to(x_half[None], (8, PIECE, HALF))
    pairs = pair_lists(codes, core)
    x_sent, padded, pairs, place = lax.optimization_barrier((x_sent, padded, pairs, place))
    x_mine = lax.all_to_all(x_sent, "rows", 0, 0).reshape(WIDTH, HALF)

    deg_part, cnt, wt = prep(padded, counts, rel_weight)
    degrees = [deg_part] + [lax.ppermute(deg_part, "cols", [(i, (i + k) % 8) for i in range(8)]) for k in range(1, 8)]
    x_mine, cnt, wt, degrees = lax.optimization_barrier((x_mine, cnt, wt, degrees))

    x_other = swap(x_mine)
    at = ((col + row) % 4 * 2 + row // 4) * (2 * BLOCK)
    x_rows = lax.dynamic_slice(x_mine, (0, at), (WIDTH, 2 * BLOCK))
    moves = [
        ((a * 8 + b) * 2 + g, (b * 8 + 4 * g + (b + a) % 4) * 2 + a // 4)
        for a in range(8)
        for b in range(8)
        for g in range(2)
    ]
    x_mine, x_rows = lax.optimization_barrier((x_mine, x_rows))
    x_own = lax.ppermute(x_rows, ("rows", "cols", "rel"), moves)
    hid = own_hidden(x_mine, wt)
    x_other, x_own, hid = lax.optimization_barrier((x_other, x_own, hid))
    to_sib, own = rest(place, padded, pairs, degrees, x_other, wt, cnt, hid)
    other = swap(to_sib)
    both = join(own, other)
    parts = lax.all_to_all(both.reshape(8, 2, WIDTH, BLOCK), "cols", 0, 0)
    return finish(parts, x_own, self_weight, bias)


def solution(mesh):
    in_specs = (
        P("cols", "rows"),
        P("rel", None, None),
        P(),
        P(),
        P("rows", "cols", "rel", None),
        P("rows", "cols", "rel", None, None, None),
    )
    out_specs = P(("rows", "cols", "rel"), None)
    return jax.shard_map(on_device, mesh=mesh, in_specs=in_specs, out_specs=out_specs, check_vma=False)
```

```python
import jax
import jax.numpy as jnp
from jax import lax
from jax.experimental import pallas as pl
from jax.experimental.pallas import tpu as pltpu
from jax.sharding import PartitionSpec as P

BLOCK = 128
WIDTH = 512
NBLK = 32
NREL = 4
SLOTS = 128
PIECE = 64
NODES = NBLK * BLOCK
HALF = NODES // 2
CHUNK = 512
UNROLL = 8
PAIRS = 72
MIB = 1024 * 1024
NT = (((1,), (1,)), ((), ()))
TN = (((0,), (0,)), ((), ()))
VMEM_SPEC = pl.BlockSpec(memory_space=pltpu.VMEM)
SMEM_SPEC = pl.BlockSpec(memory_space=pltpu.SMEM)


def params(mib):
    return pltpu.CompilerParams(vmem_limit_bytes=mib * MIB)


ANY_SPEC = pl.BlockSpec(memory_space=pl.ANY)
CHUNKS = 8
PER = SLOTS // CHUNKS


CORE, DIAGONAL = 0, 1


def counts_copies(hbm, vmem, sems):
    def copy(i):
        at = pl.ds(i * PER, PER)
        return pltpu.make_async_copy(hbm.at[at], vmem.at[at], sems.at[i])

    return copy


def prep_kernel(codes_ref, counts_hbm, weight_hbm, out_ref, wt_hbm, counts, weight, wt, deg_ref, sems):
    counts_copy = counts_copies(counts_hbm, counts, sems)
    weight_copy = pltpu.make_async_copy(weight_hbm, weight, sems.at[CHUNKS])
    wt_copy = pltpu.make_async_copy(wt, wt_hbm, sems.at[CHUNKS + 1])
    for i in range(CHUNKS):
        counts_copy(i).start()
    weight_copy.start()
    deg_ref[...] = jnp.zeros_like(deg_ref)
    ones = jnp.ones((8, BLOCK), jnp.bfloat16)

    def some(i, carry):
        counts_copy(i).wait()
        for s in range(PER):
            slot = i * PER + s
            c = counts[slot].astype(jnp.float32).astype(jnp.bfloat16)
            row = lax.dot_general(ones, c, NT, preferred_element_type=jnp.float32)
            seg = lax.shift_right_logical(codes_ref[slot], 5)
            deg_ref[pl.ds(seg, 1), :] += row[0:1]
        return carry

    lax.fori_loop(0, CHUNKS, some, 0)
    out_ref[...] = deg_ref[...].astype(jnp.bfloat16)
    weight_copy.wait()

    def turn(r, carry):
        wt[r] = weight[r].T
        return carry

    lax.fori_loop(0, NREL, turn, 0)
    wt_copy.start()
    wt_copy.wait()


def prep(codes, counts, rel_weight):
    return pl.pallas_call(
        prep_kernel,
        in_specs=[SMEM_SPEC, ANY_SPEC, ANY_SPEC],
        out_specs=[VMEM_SPEC, ANY_SPEC],
        out_shape=[
            jax.ShapeDtypeStruct((NREL * NBLK, BLOCK), jnp.bfloat16),
            jax.ShapeDtypeStruct((NREL, WIDTH, WIDTH), jnp.bfloat16),
        ],
        scratch_shapes=[
            pltpu.VMEM((SLOTS, BLOCK, BLOCK), jnp.int32),
            pltpu.VMEM((NREL, WIDTH, WIDTH), jnp.bfloat16),
            pltpu.VMEM((NREL, WIDTH, WIDTH), jnp.bfloat16),
            pltpu.VMEM((NREL * NBLK, BLOCK), jnp.float32),
            pltpu.SemaphoreType.DMA((CHUNKS + 2,)),
        ],
        compiler_params=params(52),
        cost_estimate=pl.CostEstimate(flops=2 * SLOTS * BLOCK * BLOCK * 8, bytes_accessed=12 * MIB, transcendentals=0),
        name="prep",
    )(codes, counts, rel_weight)


HALF_BLOCKS = NBLK // 2
HID = (NREL, NBLK, WIDTH, BLOCK)


def slot_pairs(codes_ref, pairs_ref, which, hid_ref, w_ref, acc_ref):
    def some(q, carry):
        for u in range(UNROLL):
            k = q * UNROLL + u
            s1, s2, place = pairs_ref[which, 0, k], pairs_ref[which, 1, k], pairs_ref[which, 2, k]
            hs = []
            for s in (s1, s2):
                code = codes_ref[s]
                hs.append(hid_ref[lax.shift_right_logical(code, 10), jnp.bitwise_and(code, NBLK - 1)])
            h = jnp.concatenate(hs, axis=1)
            w = jnp.concatenate([w_ref[s1], w_ref[s2]], axis=1)
            acc_ref[place] += lax.dot_general(h, w, NT, preferred_element_type=jnp.float32)
        return carry

    lax.fori_loop(0, pairs_ref[which, 3, 0], some, 0)


STEPS = NODES // CHUNK
PER_STEP = SLOTS // STEPS


def aggregate_kernel(place_ref, codes_ref, pairs_ref, *refs):
    deg_refs, refs = refs[:8], refs[8:]
    xm_hbm, xo_hbm, wt_hbm, counts_hbm, self_hbm, sib_hbm, own_ref, x, hid, wt, w, counts, acc, sib, inv_ref, self_w, sems = refs
    core = place_ref[CORE]
    near = STEPS // 2

    def x_copy(n, source):
        at = pl.ds(pl.multiple_of(lax.rem(n, near) * CHUNK, CHUNK), CHUNK)
        return pltpu.make_async_copy(source.at[:, at], x.at[n], sems.at[n])

    def counts_copy(n):
        at = pl.ds(n * PER_STEP, PER_STEP)
        return pltpu.make_async_copy(counts_hbm.at[at], counts.at[lax.rem(n, 4)], sems.at[STEPS + n])

    wt_copy = pltpu.make_async_copy(wt_hbm, wt, sems.at[2 * STEPS])
    sib_copy = pltpu.make_async_copy(sib, sib_hbm, sems.at[2 * STEPS + 1])
    self_copy = pltpu.make_async_copy(self_hbm, self_w, sems.at[2 * STEPS + 2])
    wt_copy.start()
    for n in range(STEPS):
        x_copy(n, xm_hbm if n < near else xo_hbm).start()
        if n < 4:
            counts_copy(n).start()

    @pl.when(place_ref[DIAGONAL] == 1)
    def _():
        self_copy.start()

    degree = deg_refs[0][...].astype(jnp.float32)
    for ref in deg_refs[1:]:
        degree = degree + ref[...].astype(jnp.float32)
    inv_ref[...] = (1.0 / jnp.maximum(degree, 1.0)).T
    w[SLOTS] = jnp.zeros((BLOCK, BLOCK), jnp.bfloat16)
    wt_copy.wait()

    def step(n, carry):
        x_copy(n, xm_hbm).wait()
        counts_copy(n).wait()
        for u in range(PER_STEP):
            slot = n * PER_STEP + u
            seg = lax.shift_right_logical(codes_ref[slot], 5)
            factor = jnp.take_along_axis(inv_ref[...], jnp.full((BLOCK, BLOCK), seg, jnp.int32), axis=1)
            w[slot] = (counts[lax.rem(n, 4), u].astype(jnp.float32) * factor).astype(jnp.bfloat16)
        zeros = jnp.zeros((HALF_BLOCKS // STEPS, WIDTH, BLOCK), jnp.float32)
        acc[pl.ds(n * (HALF_BLOCKS // STEPS), HALF_BLOCKS // STEPS)] = zeros
        own_ref[pl.ds(n * (HALF_BLOCKS // STEPS), HALF_BLOCKS // STEPS)] = zeros
        first = jnp.where(n < near, core, 1 - core) * HALF_BLOCKS + lax.rem(n, near) * (CHUNK // BLOCK)
        for r in range(NREL):
            h = jnp.dot(wt[r], x[n], preferred_element_type=jnp.float32).astype(jnp.bfloat16)
            for b in range(CHUNK // BLOCK):
                hid[r, first + b] = h[:, b * BLOCK : (b + 1) * BLOCK]

        @pl.when(n < STEPS - 4)
        def _():
            counts_copy(n + 4).start()

        return carry

    lax.fori_loop(0, STEPS, step, 0)

    @pl.when(place_ref[DIAGONAL] == 1)
    def _():
        self_copy.wait()
        turned = self_w[...].T
        for n in range(STEPS):
            cols = pl.ds(pl.multiple_of(core * (2 * BLOCK), 2 * BLOCK), 2 * BLOCK)
            term = jnp.dot(turned, x[n, :, cols], preferred_element_type=jnp.float32)
            half = core if n < near else 1 - core
            for b in range(2):
                own_ref[half * (HALF_BLOCKS // 2) + n % near * 2 + b] = term[:, b * BLOCK : (b + 1) * BLOCK]

    slot_pairs(codes_ref, pairs_ref, 0, hid, w, acc)

    def one(t, carry):
        sib[t] = acc[t].astype(jnp.bfloat16)
        return carry

    lax.fori_loop(0, HALF_BLOCKS, one, 0)
    sib_copy.start()
    slot_pairs(codes_ref, pairs_ref, 1, hid, w, own_ref)
    sib_copy.wait()


def aggregate(place, codes, pairs, degrees, x_mine, x_other, wt, counts, self_weight):
    return pl.pallas_call(
        aggregate_kernel,
        in_specs=[SMEM_SPEC] * 3 + [VMEM_SPEC] * 8 + [ANY_SPEC] * 5,
        out_specs=[ANY_SPEC, VMEM_SPEC],
        out_shape=[
            jax.ShapeDtypeStruct((HALF_BLOCKS, WIDTH, BLOCK), jnp.bfloat16),
            pltpu.VMEM((HALF_BLOCKS, WIDTH, BLOCK), jnp.float32),
        ],
        scratch_shapes=[
            pltpu.VMEM((STEPS, WIDTH, CHUNK), jnp.bfloat16),
            pltpu.VMEM(HID, jnp.bfloat16),
            pltpu.VMEM((NREL, WIDTH, WIDTH), jnp.bfloat16),
            pltpu.VMEM((SLOTS + 1, BLOCK, BLOCK), jnp.bfloat16),
            pltpu.VMEM((4, PER_STEP, BLOCK, BLOCK), jnp.int32),
            pltpu.VMEM((HALF_BLOCKS, WIDTH, BLOCK), jnp.float32),
            pltpu.VMEM((HALF_BLOCKS, WIDTH, BLOCK), jnp.bfloat16),
            pltpu.VMEM((BLOCK, BLOCK), jnp.float32),
            pltpu.VMEM((WIDTH, WIDTH), jnp.bfloat16),
            pltpu.SemaphoreType.DMA((2 * STEPS + 3,)),
        ],
        compiler_params=params(52),
        cost_estimate=pl.CostEstimate(flops=2 * NODES * WIDTH * WIDTH * NREL * 2, bytes_accessed=20 * MIB, transcendentals=0),
        name="aggregate",
    )(place, codes, pairs, *degrees, x_mine, x_other, wt, counts, self_weight)


def join_kernel(own_ref, other_ref, out_ref):
    per = out_ref.shape[0]
    step = pl.program_id(0)
    for t in range(per):
        out_ref[t] = (own_ref[step * per + t] + other_ref[t].astype(jnp.float32)).astype(jnp.bfloat16)


def join(own, other):
    spec = pl.BlockSpec((4, WIDTH, BLOCK), lambda i: (i, 0, 0))
    return pl.pallas_call(
        join_kernel,
        grid=(NBLK // 2 // 4,),
        in_specs=[VMEM_SPEC, spec],
        out_specs=spec,
        out_shape=jax.ShapeDtypeStruct((NBLK // 2, WIDTH, BLOCK), jnp.bfloat16),
        compiler_params=params(12),
        cost_estimate=pl.CostEstimate(flops=MIB, bytes_accessed=8 * MIB, transcendentals=0),
        name="join",
    )(own, other)


def finish_kernel(parts_ref, bias_ref, out_ref):
    for b in range(2):
        total = parts_ref[0, b].astype(jnp.float32)
        for k in range(1, parts_ref.shape[0]):
            total = total + parts_ref[k, b].astype(jnp.float32)
        rows = slice(b * BLOCK, (b + 1) * BLOCK)
        out_ref[rows, :] = jnp.maximum(total.T + bias_ref[...], 0.0).astype(jnp.bfloat16)


def finish(parts, bias):
    return pl.pallas_call(
        finish_kernel,
        out_shape=jax.ShapeDtypeStruct((2 * BLOCK, WIDTH), jnp.bfloat16),
        compiler_params=params(32),
        name="finish",
    )(parts, bias.reshape(1, WIDTH))


def pair_lists(codes, core):
    slots = jnp.arange(SLOTS, dtype=jnp.int32)
    target = codes // NBLK % NBLK
    half = (target // 2 % 2 == core).astype(jnp.int32)
    place = target // 4 * 2 + target % 2
    group = half * (NBLK // 2) + place
    same = group[None, :] == group[:, None]
    nth = jnp.sum((same & (slots[None, :] < slots[:, None])).astype(jnp.int32), axis=1)
    groups = jnp.arange(NBLK, dtype=jnp.int32)
    size = jnp.sum((group[None, :] == groups[:, None]).astype(jnp.int32), axis=1)
    need = (size + 1) // 2
    before = (groups[None, :] < groups[:, None]) & (groups[None, :] // (NBLK // 2) == groups[:, None] // (NBLK // 2))
    base = jnp.sum(jnp.where(before, need[None, :], 0), axis=1)
    at = half * PAIRS + nth // 2 + jnp.sum(jnp.where(group[:, None] == groups[None, :], base[None, :], 0), axis=1)
    entries = jnp.arange(2 * PAIRS, dtype=jnp.int32)
    match = at[None, :] == entries[:, None]
    is_first = match & (nth % 2 == 0)[None, :]
    is_second = match & (nth % 2 == 1)[None, :]
    first = SLOTS + jnp.sum(jnp.where(is_first, slots[None, :] - SLOTS, 0), axis=1)
    second = SLOTS + jnp.sum(jnp.where(is_second, slots[None, :] - SLOTS, 0), axis=1)
    where = jnp.sum(jnp.where(is_first, place[None, :], 0), axis=1)
    steps = (jnp.sum(need.reshape(2, NBLK // 2), axis=1) + UNROLL - 1) // UNROLL
    steps = jnp.broadcast_to(steps[:, None], (2, PAIRS))
    return jnp.stack([first.reshape(2, PAIRS), second.reshape(2, PAIRS), where.reshape(2, PAIRS), steps], axis=1)


def swap(array):
    return lax.ppermute(array, "rel", [(0, 1), (1, 0)])


def on_device(features, rel_weight, self_weight, bias, block_code, block_counts):
    row, col, core = lax.axis_index("rows"), lax.axis_index("cols"), lax.axis_index("rel")
    codes = block_code[0, 0, 0]
    counts = block_counts[0, 0, 0]

    x_half = lax.dynamic_slice(features.T, (0, core * HALF), (PIECE, HALF))
    x_sent = jnp.broadcast_to(x_half[None], (8, PIECE, HALF))
    x_sent, codes, core, row = lax.optimization_barrier((x_sent, codes, core, row))
    x_mine = lax.all_to_all(x_sent, "rows", 0, 0).reshape(WIDTH, HALF)

    padded = jnp.concatenate([codes, jnp.zeros((8,), jnp.int32)])
    place = jnp.stack([core, (row == col).astype(jnp.int32)]).astype(jnp.int32)
    pairs = pair_lists(codes, core)
    padded, place, pairs = lax.optimization_barrier((padded, place, pairs))
    deg_part, wt = prep(padded, counts, rel_weight)
    degrees = [deg_part] + [lax.ppermute(deg_part, "cols", [(i, (i + k) % 8) for i in range(8)]) for k in range(1, 8)]
    x_mine, wt, degrees = lax.optimization_barrier((x_mine, wt, degrees))

    x_other = swap(x_mine)
    to_sib, own = aggregate(place, padded, pairs, degrees, x_mine, x_other, wt, counts, self_weight)
    both = join(own, swap(to_sib))
    parts = lax.all_to_all(both.reshape(8, 2, WIDTH, BLOCK), "cols", 0, 0)
    return finish(parts, bias)


def solution(mesh):
    in_specs = (
        P("cols", "rows"),
        P("rel", None, None),
        P(),
        P(),
        P("rows", "cols", "rel", None),
        P("rows", "cols", "rel", None, None, None),
    )
    out_specs = P(("rows", "cols", "rel"), None)
    return jax.shard_map(on_device, mesh=mesh, in_specs=in_specs, out_specs=out_specs, check_vma=False)
```

```python
import jax
import jax.numpy as jnp
from jax import lax
from jax.experimental import pallas as pl
from jax.experimental.pallas import tpu as pltpu
from jax.sharding import PartitionSpec as P

BLOCK = 128
WIDTH = 512
NBLK = 32
NREL = 4
SLOTS = 128
PIECE = 64
NODES = NBLK * BLOCK
HALF = NODES // 2
CHUNK = 512
UNROLL = 8
PAIRS = 72
MIB = 1024 * 1024
NT = (((1,), (1,)), ((), ()))
TN = (((0,), (0,)), ((), ()))
VMEM_SPEC = pl.BlockSpec(memory_space=pltpu.VMEM)
SMEM_SPEC = pl.BlockSpec(memory_space=pltpu.SMEM)


def params(mib):
    return pltpu.CompilerParams(vmem_limit_bytes=mib * MIB)


ANY_SPEC = pl.BlockSpec(memory_space=pl.ANY)
CHUNKS = 8
PER = SLOTS // CHUNKS


CORE, DIAGONAL = 0, 1


def counts_copies(hbm, vmem, sems):
    def copy(i):
        at = pl.ds(i * PER, PER)
        return pltpu.make_async_copy(hbm.at[at], vmem.at[at], sems.at[i])

    return copy


def prep_kernel(codes_ref, counts_hbm, weight_hbm, out_ref, cnt_hbm, wt_hbm, counts, cnt, weight, wt, deg_ref, sems):
    counts_copy = counts_copies(counts_hbm, counts, sems)
    weight_copy = pltpu.make_async_copy(weight_hbm, weight, sems.at[CHUNKS])
    wt_copy = pltpu.make_async_copy(wt, wt_hbm, sems.at[CHUNKS + 1])
    for i in range(CHUNKS):
        counts_copy(i).start()
    weight_copy.start()
    deg_ref[...] = jnp.zeros_like(deg_ref)
    ones = jnp.ones((8, BLOCK), jnp.bfloat16)

    def cnt_copy(i):
        at = pl.ds(i * PER, PER)
        return pltpu.make_async_copy(cnt.at[at], cnt_hbm.at[at], sems.at[CHUNKS + 2 + i])

    def some(i, carry):
        counts_copy(i).wait()
        for s in range(PER):
            slot = i * PER + s
            c = counts[slot].astype(jnp.float32).astype(jnp.bfloat16)
            cnt[slot] = c
            row = lax.dot_general(ones, c, NT, preferred_element_type=jnp.float32)
            seg = lax.shift_right_logical(codes_ref[slot], 5)
            deg_ref[pl.ds(seg, 1), :] += row[0:1]
        cnt_copy(i).start()
        return carry

    lax.fori_loop(0, CHUNKS, some, 0)
    out_ref[...] = deg_ref[...].astype(jnp.bfloat16)
    weight_copy.wait()

    def turn(r, carry):
        wt[r] = weight[r].T
        return carry

    lax.fori_loop(0, NREL, turn, 0)
    wt_copy.start()
    for i in range(CHUNKS):
        cnt_copy(i).wait()
    wt_copy.wait()


def prep(codes, counts, rel_weight):
    return pl.pallas_call(
        prep_kernel,
        in_specs=[SMEM_SPEC, ANY_SPEC, ANY_SPEC],
        out_specs=[VMEM_SPEC, ANY_SPEC, ANY_SPEC],
        out_shape=[
            jax.ShapeDtypeStruct((NREL * NBLK, BLOCK), jnp.bfloat16),
            jax.ShapeDtypeStruct((SLOTS, BLOCK, BLOCK), jnp.bfloat16),
            jax.ShapeDtypeStruct((NREL, WIDTH, WIDTH), jnp.bfloat16),
        ],
        scratch_shapes=[
            pltpu.VMEM((SLOTS, BLOCK, BLOCK), jnp.int32),
            pltpu.VMEM((SLOTS, BLOCK, BLOCK), jnp.bfloat16),
            pltpu.VMEM((NREL, WIDTH, WIDTH), jnp.bfloat16),
            pltpu.VMEM((NREL, WIDTH, WIDTH), jnp.bfloat16),
            pltpu.VMEM((NREL * NBLK, BLOCK), jnp.float32),
            pltpu.SemaphoreType.DMA((2 * CHUNKS + 2,)),
        ],
        compiler_params=params(52),
        cost_estimate=pl.CostEstimate(flops=2 * SLOTS * BLOCK * BLOCK * 8, bytes_accessed=12 * MIB, transcendentals=0),
        name="prep",
    )(codes, counts, rel_weight)


HALF_BLOCKS = NBLK // 2
HID = (NREL, NBLK, WIDTH, BLOCK)


def slot_pairs(codes_ref, pairs_ref, which, hid_ref, w_ref, acc_ref):
    def some(q, carry):
        for u in range(UNROLL):
            k = q * UNROLL + u
            s1, s2, place = pairs_ref[which, 0, k], pairs_ref[which, 1, k], pairs_ref[which, 2, k]
            hs = []
            for s in (s1, s2):
                code = codes_ref[s]
                hs.append(hid_ref[lax.shift_right_logical(code, 10), jnp.bitwise_and(code, NBLK - 1)])
            h = jnp.concatenate(hs, axis=1)
            w = jnp.concatenate([w_ref[s1], w_ref[s2]], axis=1)
            acc_ref[place] += lax.dot_general(h, w, NT, preferred_element_type=jnp.float32)
        return carry

    lax.fori_loop(0, pairs_ref[which, 3, 0], some, 0)


STEPS = NODES // CHUNK
PER_STEP = SLOTS // STEPS


def load_kernel(*refs):
    deg_refs, (wt_hbm, cnt_hbm, wt_ref, cnt_ref, inv_ref, sems) = refs[:8], refs[8:]
    copies = [pltpu.make_async_copy(wt_hbm, wt_ref, sems.at[0]), pltpu.make_async_copy(cnt_hbm, cnt_ref, sems.at[1])]
    for copy in copies:
        copy.start()
    degree = deg_refs[0][...].astype(jnp.float32)
    for ref in deg_refs[1:]:
        degree = degree + ref[...].astype(jnp.float32)
    inv_ref[...] = (1.0 / jnp.maximum(degree, 1.0)).T
    for copy in copies:
        copy.wait()


def load(degrees, wt, cnt):
    return pl.pallas_call(
        load_kernel,
        in_specs=[VMEM_SPEC] * 8 + [ANY_SPEC] * 2,
        out_specs=[VMEM_SPEC] * 3,
        out_shape=[
            pltpu.VMEM(wt.shape, wt.dtype),
            pltpu.VMEM(cnt.shape, cnt.dtype),
            pltpu.VMEM((BLOCK, NREL * NBLK), jnp.float32),
        ],
        scratch_shapes=[pltpu.SemaphoreType.DMA((2,))],
        compiler_params=params(12),
        cost_estimate=pl.CostEstimate(flops=1, bytes_accessed=12 * MIB, transcendentals=0),
        name="load",
    )(*degrees, wt, cnt)


def here(*arrays):
    return [pltpu.with_memory_space_constraint(a, pltpu.VMEM) for a in arrays]


def sibling_kernel(place_ref, codes_ref, pairs_ref, inv_ref, xm_ref, xo_ref, wt, cnt, sib_ref, hid, w, acc):
    core = place_ref[CORE]
    near = STEPS // 2
    w[SLOTS] = jnp.zeros((BLOCK, BLOCK), jnp.bfloat16)

    for k, x_ref in enumerate((xm_ref, xo_ref)):

        def step(i, carry):
            n = k * near + i
            first = (core, 1 - core)[k] * HALF_BLOCKS + i * (CHUNK // BLOCK)
            x = x_ref[:, pl.ds(pl.multiple_of(i * CHUNK, CHUNK), CHUNK)]
            for r in range(NREL):
                h = jnp.dot(wt[r], x, preferred_element_type=jnp.float32).astype(jnp.bfloat16)
                for u in range(r * PER_STEP // NREL, (r + 1) * PER_STEP // NREL):
                    slot = n * PER_STEP + u
                    seg = lax.shift_right_logical(codes_ref[slot], 5)
                    factor = jnp.take_along_axis(inv_ref[...], jnp.full((BLOCK, BLOCK), seg, jnp.int32), axis=1)
                    w[slot] = (cnt[slot].astype(jnp.float32) * factor).astype(jnp.bfloat16)
                for b in range(CHUNK // BLOCK):
                    hid[r, first + b] = h[:, b * BLOCK : (b + 1) * BLOCK]
            for t in range(HALF_BLOCKS // STEPS):
                acc[n * (HALF_BLOCKS // STEPS) + t] = jnp.zeros((WIDTH, BLOCK), jnp.float32)
            return carry

        lax.fori_loop(0, near, step, 0)

    slot_pairs(codes_ref, pairs_ref, 0, hid, w, acc)

    def one(t, carry):
        sib_ref[t] = acc[t].astype(jnp.bfloat16)
        return carry

    lax.fori_loop(0, HALF_BLOCKS, one, 0)


def sibling_part(place, codes, pairs, inverse, x_mine, x_other, wt, cnt):
    return pl.pallas_call(
        sibling_kernel,
        in_specs=[SMEM_SPEC] * 3 + [VMEM_SPEC] * 5,
        out_specs=[VMEM_SPEC] * 3,
        out_shape=[
            pltpu.VMEM((HALF_BLOCKS, WIDTH, BLOCK), jnp.bfloat16),
            pltpu.VMEM(HID, jnp.bfloat16),
            pltpu.VMEM((SLOTS + 1, BLOCK, BLOCK), jnp.bfloat16),
        ],
        scratch_shapes=[pltpu.VMEM((HALF_BLOCKS, WIDTH, BLOCK), jnp.float32)],
        compiler_params=params(12),
        cost_estimate=pl.CostEstimate(flops=2 * NODES * WIDTH * WIDTH * NREL, bytes_accessed=20 * MIB, transcendentals=0),
        name="sibling_part",
    )(place, codes, pairs, *here(inverse, x_mine, x_other, wt, cnt))


def own_kernel(place_ref, codes_ref, pairs_ref, xm_ref, xo_ref, self_hbm, hid, w, own_ref, self_w, sems):
    core = place_ref[CORE]
    self_copy = pltpu.make_async_copy(self_hbm, self_w, sems.at[0])

    @pl.when(place_ref[DIAGONAL] == 0)
    def _():
        def one(t, carry):
            own_ref[t] = jnp.zeros((WIDTH, BLOCK), jnp.float32)
            return carry

        lax.fori_loop(0, HALF_BLOCKS, one, 0)

    @pl.when(place_ref[DIAGONAL] == 1)
    def _():
        self_copy.start()
        self_copy.wait()
        turned = self_w[...].T
        for half, x_ref in ((core, xm_ref), (1 - core, xo_ref)):
            for q in range(HALF_BLOCKS // 4):
                at = pl.multiple_of(core * (2 * BLOCK) + q * (4 * BLOCK), 2 * BLOCK)
                term = jnp.dot(turned, x_ref[:, pl.ds(at, 2 * BLOCK)], preferred_element_type=jnp.float32)
                for b in range(2):
                    own_ref[half * (HALF_BLOCKS // 2) + q * 2 + b] = term[:, b * BLOCK : (b + 1) * BLOCK]

    slot_pairs(codes_ref, pairs_ref, 1, hid, w, own_ref)


def own_part(place, codes, pairs, x_mine, x_other, self_weight, hid, w):
    x_mine, x_other, hid, w = here(x_mine, x_other, hid, w)
    return pl.pallas_call(
        own_kernel,
        in_specs=[SMEM_SPEC] * 3 + [VMEM_SPEC] * 2 + [ANY_SPEC] + [VMEM_SPEC] * 2,
        out_specs=VMEM_SPEC,
        out_shape=pltpu.VMEM((HALF_BLOCKS, WIDTH, BLOCK), jnp.float32),
        scratch_shapes=[pltpu.VMEM((WIDTH, WIDTH), jnp.bfloat16), pltpu.SemaphoreType.DMA((1,))],
        compiler_params=params(12),
        cost_estimate=pl.CostEstimate(flops=2 * HALF * WIDTH * WIDTH * NREL, bytes_accessed=20 * MIB, transcendentals=0),
        name="own_part",
    )(place, codes, pairs, x_mine, x_other, self_weight, hid, w)


def join_kernel(own_ref, other_ref, out_ref):
    per = out_ref.shape[0]
    step = pl.program_id(0)
    for t in range(per):
        out_ref[t] = (own_ref[step * per + t] + other_ref[t].astype(jnp.float32)).astype(jnp.bfloat16)


def join(own, other):
    spec = pl.BlockSpec((4, WIDTH, BLOCK), lambda i: (i, 0, 0))
    return pl.pallas_call(
        join_kernel,
        grid=(NBLK // 2 // 4,),
        in_specs=[VMEM_SPEC, spec],
        out_specs=spec,
        out_shape=jax.ShapeDtypeStruct((NBLK // 2, WIDTH, BLOCK), jnp.bfloat16),
        compiler_params=params(12),
        cost_estimate=pl.CostEstimate(flops=MIB, bytes_accessed=8 * MIB, transcendentals=0),
        name="join",
    )(own, other)


def finish_kernel(parts_ref, bias_ref, out_ref):
    for b in range(2):
        total = parts_ref[0, b].astype(jnp.float32)
        for k in range(1, parts_ref.shape[0]):
            total = total + parts_ref[k, b].astype(jnp.float32)
        rows = slice(b * BLOCK, (b + 1) * BLOCK)
        out_ref[rows, :] = jnp.maximum(total.T + bias_ref[...], 0.0).astype(jnp.bfloat16)


def finish(parts, bias):
    return pl.pallas_call(
        finish_kernel,
        out_shape=jax.ShapeDtypeStruct((2 * BLOCK, WIDTH), jnp.bfloat16),
        compiler_params=params(32),
        name="finish",
    )(parts, bias.reshape(1, WIDTH))


def pair_lists(codes, core):
    slots = jnp.arange(SLOTS, dtype=jnp.int32)
    target = codes // NBLK % NBLK
    half = (target // 2 % 2 == core).astype(jnp.int32)
    place = target // 4 * 2 + target % 2
    group = half * (NBLK // 2) + place
    same = group[None, :] == group[:, None]
    nth = jnp.sum((same & (slots[None, :] < slots[:, None])).astype(jnp.int32), axis=1)
    groups = jnp.arange(NBLK, dtype=jnp.int32)
    size = jnp.sum((group[None, :] == groups[:, None]).astype(jnp.int32), axis=1)
    need = (size + 1) // 2
    before = (groups[None, :] < groups[:, None]) & (groups[None, :] // (NBLK // 2) == groups[:, None] // (NBLK // 2))
    base = jnp.sum(jnp.where(before, need[None, :], 0), axis=1)
    at = half * PAIRS + nth // 2 + jnp.sum(jnp.where(group[:, None] == groups[None, :], base[None, :], 0), axis=1)
    entries = jnp.arange(2 * PAIRS, dtype=jnp.int32)
    match = at[None, :] == entries[:, None]
    is_first = match & (nth % 2 == 0)[None, :]
    is_second = match & (nth % 2 == 1)[None, :]
    first = SLOTS + jnp.sum(jnp.where(is_first, slots[None, :] - SLOTS, 0), axis=1)
    second = SLOTS + jnp.sum(jnp.where(is_second, slots[None, :] - SLOTS, 0), axis=1)
    where = jnp.sum(jnp.where(is_first, place[None, :], 0), axis=1)
    steps = (jnp.sum(need.reshape(2, NBLK // 2), axis=1) + UNROLL - 1) // UNROLL
    steps = jnp.broadcast_to(steps[:, None], (2, PAIRS))
    return jnp.stack([first.reshape(2, PAIRS), second.reshape(2, PAIRS), where.reshape(2, PAIRS), steps], axis=1)


def swap(array):
    return lax.ppermute(array, "rel", [(0, 1), (1, 0)])


def on_device(features, rel_weight, self_weight, bias, block_code, block_counts):
    row, col, core = lax.axis_index("rows"), lax.axis_index("cols"), lax.axis_index("rel")
    codes = block_code[0, 0, 0]
    counts = block_counts[0, 0, 0]

    x_half = lax.dynamic_slice(features.T, (0, core * HALF), (PIECE, HALF))
    x_sent = jnp.broadcast_to(x_half[None], (8, PIECE, HALF))
    x_sent, codes, core, row = lax.optimization_barrier((x_sent, codes, core, row))
    x_mine = lax.all_to_all(x_sent, "rows", 0, 0).reshape(WIDTH, HALF)

    padded = jnp.concatenate([codes, jnp.zeros((8,), jnp.int32)])
    place = jnp.stack([core, (row == col).astype(jnp.int32)]).astype(jnp.int32)
    pairs = pair_lists(codes, core)
    padded, place, pairs = lax.optimization_barrier((padded, place, pairs))
    deg_part, cnt, wt = prep(padded, counts, rel_weight)
    degrees = [deg_part] + [lax.ppermute(deg_part, "cols", [(i, (i + k) % 8) for i in range(8)]) for k in range(1, 8)]
    x_mine, cnt, wt, degrees = lax.optimization_barrier((x_mine, cnt, wt, degrees))

    x_other = swap(x_mine)
    wt, cnt, inverse = load(degrees, wt, cnt)
    to_sib, hid, w = sibling_part(place, padded, pairs, inverse, x_mine, x_other, wt, cnt)
    other = swap(to_sib)
    own = own_part(place, padded, pairs, x_mine, x_other, self_weight, hid, w)
    both = join(own, other)
    parts = lax.all_to_all(both.reshape(8, 2, WIDTH, BLOCK), "cols", 0, 0)
    return finish(parts, bias)


def solution(mesh):
    in_specs = (
        P("cols", "rows"),
        P("rel", None, None),
        P(),
        P(),
        P("rows", "cols", "rel", None),
        P("rows", "cols", "rel", None, None, None),
    )
    out_specs = P(("rows", "cols", "rel"), None)
    return jax.shard_map(on_device, mesh=mesh, in_specs=in_specs, out_specs=out_specs, check_vma=False)
```

```python
import jax
import jax.numpy as jnp
from jax import lax
from jax.experimental import pallas as pl
from jax.experimental.pallas import tpu as pltpu
from jax.sharding import PartitionSpec as P

BLOCK = 128
WIDTH = 512
NBLK = 32
NREL = 4
SLOTS = 128
PIECE = 64
NODES = NBLK * BLOCK
HALF = NODES // 2
CHUNK = 512
UNROLL = 8
PAIRS = 72
MIB = 1024 * 1024
NT = (((1,), (1,)), ((), ()))
TN = (((0,), (0,)), ((), ()))
VMEM_SPEC = pl.BlockSpec(memory_space=pltpu.VMEM)
SMEM_SPEC = pl.BlockSpec(memory_space=pltpu.SMEM)


def params(mib):
    return pltpu.CompilerParams(vmem_limit_bytes=mib * MIB)


ANY_SPEC = pl.BlockSpec(memory_space=pl.ANY)
CHUNKS = 8
PER = SLOTS // CHUNKS


CORE, DIAGONAL = 0, 1


def counts_copies(hbm, vmem, sems):
    def copy(i):
        at = pl.ds(i * PER, PER)
        return pltpu.make_async_copy(hbm.at[at], vmem.at[at], sems.at[i])

    return copy


def prep_kernel(codes_ref, counts_hbm, weight_hbm, out_ref, cnt_hbm, wt_hbm, counts, cnt, weight, wt, deg_ref, sems):
    counts_copy = counts_copies(counts_hbm, counts, sems)
    weight_copy = pltpu.make_async_copy(weight_hbm, weight, sems.at[CHUNKS])
    wt_copy = pltpu.make_async_copy(wt, wt_hbm, sems.at[CHUNKS + 1])
    for i in range(CHUNKS):
        counts_copy(i).start()
    weight_copy.start()
    deg_ref[...] = jnp.zeros_like(deg_ref)
    ones = jnp.ones((8, BLOCK), jnp.bfloat16)

    def cnt_copy(i):
        at = pl.ds(i * PER, PER)
        return pltpu.make_async_copy(cnt.at[at], cnt_hbm.at[at], sems.at[CHUNKS + 2 + i])

    def some(i, carry):
        counts_copy(i).wait()
        for s in range(PER):
            slot = i * PER + s
            c = counts[slot].astype(jnp.float32).astype(jnp.bfloat16)
            cnt[slot] = c
            row = lax.dot_general(ones, c, NT, preferred_element_type=jnp.float32)
            seg = lax.shift_right_logical(codes_ref[slot], 5)
            deg_ref[pl.ds(seg, 1), :] += row[0:1]
        cnt_copy(i).start()
        return carry

    lax.fori_loop(0, CHUNKS, some, 0)
    out_ref[...] = deg_ref[...].astype(jnp.bfloat16)
    weight_copy.wait()

    def turn(r, carry):
        wt[r] = weight[r].T
        return carry

    lax.fori_loop(0, NREL, turn, 0)
    wt_copy.start()
    for i in range(CHUNKS):
        cnt_copy(i).wait()
    wt_copy.wait()


def prep(codes, counts, rel_weight):
    return pl.pallas_call(
        prep_kernel,
        in_specs=[SMEM_SPEC, ANY_SPEC, ANY_SPEC],
        out_specs=[VMEM_SPEC, ANY_SPEC, ANY_SPEC],
        out_shape=[
            jax.ShapeDtypeStruct((NREL * NBLK, BLOCK), jnp.bfloat16),
            jax.ShapeDtypeStruct((SLOTS, BLOCK, BLOCK), jnp.bfloat16),
            jax.ShapeDtypeStruct((NREL, WIDTH, WIDTH), jnp.bfloat16),
        ],
        scratch_shapes=[
            pltpu.VMEM((SLOTS, BLOCK, BLOCK), jnp.int32),
            pltpu.VMEM((SLOTS, BLOCK, BLOCK), jnp.bfloat16),
            pltpu.VMEM((NREL, WIDTH, WIDTH), jnp.bfloat16),
            pltpu.VMEM((NREL, WIDTH, WIDTH), jnp.bfloat16),
            pltpu.VMEM((NREL * NBLK, BLOCK), jnp.float32),
            pltpu.SemaphoreType.DMA((2 * CHUNKS + 2,)),
        ],
        compiler_params=params(52),
        cost_estimate=pl.CostEstimate(flops=2 * SLOTS * BLOCK * BLOCK * 8, bytes_accessed=12 * MIB, transcendentals=0),
        name="prep",
    )(codes, counts, rel_weight)


HALF_BLOCKS = NBLK // 2
HID = (NREL, NBLK, WIDTH, BLOCK)


def slot_pairs(codes_ref, pairs_ref, which, hid_ref, w_ref, acc_ref):
    def some(q, carry):
        for u in range(UNROLL):
            k = q * UNROLL + u
            s1, s2, place = pairs_ref[which, 0, k], pairs_ref[which, 1, k], pairs_ref[which, 2, k]
            hs = []
            for s in (s1, s2):
                code = codes_ref[s]
                hs.append(hid_ref[lax.shift_right_logical(code, 10), jnp.bitwise_and(code, NBLK - 1)])
            h = jnp.concatenate(hs, axis=1)
            w = jnp.concatenate([w_ref[s1], w_ref[s2]], axis=1)
            acc_ref[place] += lax.dot_general(h, w, NT, preferred_element_type=jnp.float32)
        return carry

    lax.fori_loop(0, pairs_ref[which, 3, 0], some, 0)


STEPS = NODES // CHUNK
PER_STEP = SLOTS // STEPS


def load_kernel(*refs):
    deg_refs, (place_ref, x_ref, wt_hbm, cnt_hbm, wt_ref, cnt_ref, inv_ref, hid, sems) = refs[:8], refs[8:]
    copies = [pltpu.make_async_copy(wt_hbm, wt_ref, sems.at[0]), pltpu.make_async_copy(cnt_hbm, cnt_ref, sems.at[1])]
    for copy in copies:
        copy.start()
    degree = deg_refs[0][...].astype(jnp.float32)
    for ref in deg_refs[1:]:
        degree = degree + ref[...].astype(jnp.float32)
    inv_ref[...] = (1.0 / jnp.maximum(degree, 1.0)).T
    copies[0].wait()

    def step(i, carry):
        first = place_ref[CORE] * HALF_BLOCKS + i * (CHUNK // BLOCK)
        x = x_ref[:, pl.ds(pl.multiple_of(i * CHUNK, CHUNK), CHUNK)]
        for r in range(NREL):
            h = jnp.dot(wt_ref[r], x, preferred_element_type=jnp.float32).astype(jnp.bfloat16)
            for b in range(CHUNK // BLOCK):
                hid[r, first + b] = h[:, b * BLOCK : (b + 1) * BLOCK]
        return carry

    lax.fori_loop(0, STEPS // 2, step, 0)
    copies[1].wait()


def load(degrees, place, x_mine, wt, cnt):
    return pl.pallas_call(
        load_kernel,
        in_specs=[VMEM_SPEC] * 8 + [SMEM_SPEC, VMEM_SPEC] + [ANY_SPEC] * 2,
        out_specs=[VMEM_SPEC] * 4,
        out_shape=[
            pltpu.VMEM(wt.shape, wt.dtype),
            pltpu.VMEM(cnt.shape, cnt.dtype),
            pltpu.VMEM((BLOCK, NREL * NBLK), jnp.float32),
            pltpu.VMEM(HID, jnp.bfloat16),
        ],
        scratch_shapes=[pltpu.SemaphoreType.DMA((2,))],
        compiler_params=params(28),
        cost_estimate=pl.CostEstimate(flops=NODES * WIDTH * WIDTH * NREL, bytes_accessed=12 * MIB, transcendentals=0),
        name="own_hidden",
    )(*degrees, place, *here(x_mine), wt, cnt)


def here(*arrays):
    return [pltpu.with_memory_space_constraint(a, pltpu.VMEM) for a in arrays]


def sibling_kernel(place_ref, codes_ref, pairs_ref, inv_ref, x_ref, wt, cnt, hid_in, sib_ref, hid, w, acc):
    core = place_ref[CORE]
    w[SLOTS] = jnp.zeros((BLOCK, BLOCK), jnp.bfloat16)
    per_step = 2 * PER_STEP
    clear = 2 * HALF_BLOCKS // STEPS

    def step(i, carry):
        first = (1 - core) * HALF_BLOCKS + i * (CHUNK // BLOCK)
        x = x_ref[:, pl.ds(pl.multiple_of(i * CHUNK, CHUNK), CHUNK)]
        for r in range(NREL):
            h = jnp.dot(wt[r], x, preferred_element_type=jnp.float32).astype(jnp.bfloat16)
            for u in range(r * per_step // NREL, (r + 1) * per_step // NREL):
                slot = i * per_step + u
                seg = lax.shift_right_logical(codes_ref[slot], 5)
                factor = jnp.take_along_axis(inv_ref[...], jnp.full((BLOCK, BLOCK), seg, jnp.int32), axis=1)
                w[slot] = (cnt[slot].astype(jnp.float32) * factor).astype(jnp.bfloat16)
            for b in range(CHUNK // BLOCK):
                hid[r, first + b] = h[:, b * BLOCK : (b + 1) * BLOCK]
        for t in range(clear):
            acc[i * clear + t] = jnp.zeros((WIDTH, BLOCK), jnp.float32)
        return carry

    lax.fori_loop(0, STEPS // 2, step, 0)
    slot_pairs(codes_ref, pairs_ref, 0, hid, w, acc)

    def one(t, carry):
        sib_ref[t] = acc[t].astype(jnp.bfloat16)
        return carry

    lax.fori_loop(0, HALF_BLOCKS, one, 0)


def sibling_part(place, codes, pairs, inverse, x_other, wt, cnt, hid):
    return pl.pallas_call(
        sibling_kernel,
        in_specs=[SMEM_SPEC] * 3 + [VMEM_SPEC] * 5,
        out_specs=[VMEM_SPEC] * 3,
        out_shape=[
            pltpu.VMEM((HALF_BLOCKS, WIDTH, BLOCK), jnp.bfloat16),
            pltpu.VMEM(HID, jnp.bfloat16),
            pltpu.VMEM((SLOTS + 1, BLOCK, BLOCK), jnp.bfloat16),
        ],
        input_output_aliases={7: 1},
        scratch_shapes=[pltpu.VMEM((HALF_BLOCKS, WIDTH, BLOCK), jnp.float32)],
        compiler_params=params(12),
        cost_estimate=pl.CostEstimate(flops=2 * NODES * WIDTH * WIDTH * NREL, bytes_accessed=20 * MIB, transcendentals=0),
        name="sibling_part",
    )(place, codes, pairs, *here(inverse, x_other, wt, cnt, hid))


def own_kernel(place_ref, codes_ref, pairs_ref, xm_ref, xo_ref, self_ref, hid, w, own_ref):
    core = place_ref[CORE]

    @pl.when(place_ref[DIAGONAL] == 0)
    def _():
        def one(t, carry):
            own_ref[t] = jnp.zeros((WIDTH, BLOCK), jnp.float32)
            return carry

        lax.fori_loop(0, HALF_BLOCKS, one, 0)

    @pl.when(place_ref[DIAGONAL] == 1)
    def _():
        turned = self_ref[...].T
        for half, x_ref in ((core, xm_ref), (1 - core, xo_ref)):
            for q in range(HALF_BLOCKS // 4):
                at = pl.multiple_of(core * (2 * BLOCK) + q * (4 * BLOCK), 2 * BLOCK)
                term = jnp.dot(turned, x_ref[:, pl.ds(at, 2 * BLOCK)], preferred_element_type=jnp.float32)
                for b in range(2):
                    own_ref[half * (HALF_BLOCKS // 2) + q * 2 + b] = term[:, b * BLOCK : (b + 1) * BLOCK]

    slot_pairs(codes_ref, pairs_ref, 1, hid, w, own_ref)


def own_part(place, codes, pairs, x_mine, x_other, self_weight, hid, w):
    x_mine, x_other, hid, w = here(x_mine, x_other, hid, w)
    return pl.pallas_call(
        own_kernel,
        in_specs=[SMEM_SPEC] * 3 + [VMEM_SPEC] * 5,
        out_specs=VMEM_SPEC,
        out_shape=pltpu.VMEM((HALF_BLOCKS, WIDTH, BLOCK), jnp.float32),
        compiler_params=params(12),
        cost_estimate=pl.CostEstimate(flops=2 * HALF * WIDTH * WIDTH * NREL, bytes_accessed=20 * MIB, transcendentals=0),
        name="own_part",
    )(place, codes, pairs, x_mine, x_other, self_weight, hid, w)


def join_kernel(own_ref, other_ref, out_ref):
    per = out_ref.shape[0]
    step = pl.program_id(0)
    for t in range(per):
        out_ref[t] = (own_ref[step * per + t] + other_ref[t].astype(jnp.float32)).astype(jnp.bfloat16)


def join(own, other):
    spec = pl.BlockSpec((4, WIDTH, BLOCK), lambda i: (i, 0, 0))
    return pl.pallas_call(
        join_kernel,
        grid=(NBLK // 2 // 4,),
        in_specs=[VMEM_SPEC, spec],
        out_specs=spec,
        out_shape=jax.ShapeDtypeStruct((NBLK // 2, WIDTH, BLOCK), jnp.bfloat16),
        compiler_params=params(12),
        cost_estimate=pl.CostEstimate(flops=MIB, bytes_accessed=8 * MIB, transcendentals=0),
        name="join",
    )(own, other)


def finish_kernel(parts_ref, bias_ref, out_ref):
    for b in range(2):
        total = parts_ref[0, b].astype(jnp.float32)
        for k in range(1, parts_ref.shape[0]):
            total = total + parts_ref[k, b].astype(jnp.float32)
        rows = slice(b * BLOCK, (b + 1) * BLOCK)
        out_ref[rows, :] = jnp.maximum(total.T + bias_ref[...], 0.0).astype(jnp.bfloat16)


def finish(parts, bias):
    return pl.pallas_call(
        finish_kernel,
        out_shape=jax.ShapeDtypeStruct((2 * BLOCK, WIDTH), jnp.bfloat16),
        compiler_params=params(32),
        name="finish",
    )(parts, bias.reshape(1, WIDTH))


def pair_lists(codes, core):
    slots = jnp.arange(SLOTS, dtype=jnp.int32)
    target = codes // NBLK % NBLK
    half = (target // 2 % 2 == core).astype(jnp.int32)
    place = target // 4 * 2 + target % 2
    group = half * (NBLK // 2) + place
    same = group[None, :] == group[:, None]
    nth = jnp.sum((same & (slots[None, :] < slots[:, None])).astype(jnp.int32), axis=1)
    groups = jnp.arange(NBLK, dtype=jnp.int32)
    size = jnp.sum((group[None, :] == groups[:, None]).astype(jnp.int32), axis=1)
    need = (size + 1) // 2
    before = (groups[None, :] < groups[:, None]) & (groups[None, :] // (NBLK // 2) == groups[:, None] // (NBLK // 2))
    base = jnp.sum(jnp.where(before, need[None, :], 0), axis=1)
    at = half * PAIRS + nth // 2 + jnp.sum(jnp.where(group[:, None] == groups[None, :], base[None, :], 0), axis=1)
    entries = jnp.arange(2 * PAIRS, dtype=jnp.int32)
    match = at[None, :] == entries[:, None]
    is_first = match & (nth % 2 == 0)[None, :]
    is_second = match & (nth % 2 == 1)[None, :]
    first = SLOTS + jnp.sum(jnp.where(is_first, slots[None, :] - SLOTS, 0), axis=1)
    second = SLOTS + jnp.sum(jnp.where(is_second, slots[None, :] - SLOTS, 0), axis=1)
    where = jnp.sum(jnp.where(is_first, place[None, :], 0), axis=1)
    steps = (jnp.sum(need.reshape(2, NBLK // 2), axis=1) + UNROLL - 1) // UNROLL
    steps = jnp.broadcast_to(steps[:, None], (2, PAIRS))
    return jnp.stack([first.reshape(2, PAIRS), second.reshape(2, PAIRS), where.reshape(2, PAIRS), steps], axis=1)


def swap(array):
    return lax.ppermute(array, "rel", [(0, 1), (1, 0)])


def on_device(features, rel_weight, self_weight, bias, block_code, block_counts):
    row, col, core = lax.axis_index("rows"), lax.axis_index("cols"), lax.axis_index("rel")
    codes = block_code[0, 0, 0]
    counts = block_counts[0, 0, 0]

    x_half = lax.dynamic_slice(features.T, (0, core * HALF), (PIECE, HALF))
    x_sent = jnp.broadcast_to(x_half[None], (8, PIECE, HALF))
    x_sent, codes, core, row = lax.optimization_barrier((x_sent, codes, core, row))
    x_mine = lax.all_to_all(x_sent, "rows", 0, 0).reshape(WIDTH, HALF)

    padded = jnp.concatenate([codes, jnp.zeros((8,), jnp.int32)])
    place = jnp.stack([core, (row == col).astype(jnp.int32)]).astype(jnp.int32)
    pairs = pair_lists(codes, core)
    padded, place, pairs = lax.optimization_barrier((padded, place, pairs))
    deg_part, cnt, wt = prep(padded, counts, rel_weight)
    degrees = [deg_part] + [lax.ppermute(deg_part, "cols", [(i, (i + k) % 8) for i in range(8)]) for k in range(1, 8)]
    x_mine, cnt, wt, degrees = lax.optimization_barrier((x_mine, cnt, wt, degrees))

    x_other = swap(x_mine)
    wt, cnt, inverse, hid = load(degrees, place, x_mine, wt, cnt)
    to_sib, hid, w = sibling_part(place, padded, pairs, inverse, x_other, wt, cnt, hid)
    other = swap(to_sib)
    own = own_part(place, padded, pairs, x_mine, x_other, self_weight, hid, w)
    both = join(own, other)
    parts = lax.all_to_all(both.reshape(8, 2, WIDTH, BLOCK), "cols", 0, 0)
    return finish(parts, bias)


def solution(mesh):
    in_specs = (
        P("cols", "rows"),
        P("rel", None, None),
        P(),
        P(),
        P("rows", "cols", "rel", None),
        P("rows", "cols", "rel", None, None, None),
    )
    out_specs = P(("rows", "cols", "rel"), None)
    return jax.shard_map(on_device, mesh=mesh, in_specs=in_specs, out_specs=out_specs, check_vma=False)
```

```python
import jax
import jax.numpy as jnp
from jax import lax
from jax.experimental import pallas as pl
from jax.experimental.pallas import tpu as pltpu
from jax.sharding import PartitionSpec as P

BLOCK = 128
WIDTH = 512
NBLK = 32
NREL = 4
SLOTS = 128
PIECE = 64
NODES = NBLK * BLOCK
HALF = NODES // 2
CHUNK = 512
UNROLL = 8
PAIRS = 72
MIB = 1024 * 1024
NT = (((1,), (1,)), ((), ()))
TN = (((0,), (0,)), ((), ()))
VMEM_SPEC = pl.BlockSpec(memory_space=pltpu.VMEM)
SMEM_SPEC = pl.BlockSpec(memory_space=pltpu.SMEM)


def params(mib):
    return pltpu.CompilerParams(vmem_limit_bytes=mib * MIB)


ANY_SPEC = pl.BlockSpec(memory_space=pl.ANY)
CHUNKS = 8
PER = SLOTS // CHUNKS


CORE, DIAGONAL = 0, 1


def counts_copies(hbm, vmem, sems):
    def copy(i):
        at = pl.ds(i * PER, PER)
        return pltpu.make_async_copy(hbm.at[at], vmem.at[at], sems.at[i])

    return copy


def prep_kernel(codes_ref, counts_hbm, weight_hbm, out_ref, cnt_hbm, wt_hbm, counts, cnt, weight, wt, deg_ref, sems):
    counts_copy = counts_copies(counts_hbm, counts, sems)
    weight_copy = pltpu.make_async_copy(weight_hbm, weight, sems.at[CHUNKS])
    wt_copy = pltpu.make_async_copy(wt, wt_hbm, sems.at[CHUNKS + 1])
    for i in range(CHUNKS):
        counts_copy(i).start()
    weight_copy.start()
    deg_ref[...] = jnp.zeros_like(deg_ref)
    ones = jnp.ones((8, BLOCK), jnp.bfloat16)

    def cnt_copy(i):
        at = pl.ds(i * PER, PER)
        return pltpu.make_async_copy(cnt.at[at], cnt_hbm.at[at], sems.at[CHUNKS + 2 + i])

    def some(i, carry):
        counts_copy(i).wait()
        for s in range(PER):
            slot = i * PER + s
            c = counts[slot].astype(jnp.float32).astype(jnp.bfloat16)
            cnt[slot] = c
            row = lax.dot_general(ones, c, NT, preferred_element_type=jnp.float32)
            seg = lax.shift_right_logical(codes_ref[slot], 5)
            deg_ref[pl.ds(seg, 1), :] += row[0:1]
        cnt_copy(i).start()
        return carry

    lax.fori_loop(0, CHUNKS, some, 0)
    out_ref[...] = deg_ref[...].astype(jnp.bfloat16)
    weight_copy.wait()

    def turn(r, carry):
        wt[r] = weight[r].T
        return carry

    lax.fori_loop(0, NREL, turn, 0)
    wt_copy.start()
    for i in range(CHUNKS):
        cnt_copy(i).wait()
    wt_copy.wait()


def prep(codes, counts, rel_weight):
    return pl.pallas_call(
        prep_kernel,
        in_specs=[SMEM_SPEC, ANY_SPEC, ANY_SPEC],
        out_specs=[VMEM_SPEC, ANY_SPEC, ANY_SPEC],
        out_shape=[
            jax.ShapeDtypeStruct((NREL * NBLK, BLOCK), jnp.bfloat16),
            jax.ShapeDtypeStruct((SLOTS, BLOCK, BLOCK), jnp.bfloat16),
            jax.ShapeDtypeStruct((NREL, WIDTH, WIDTH), jnp.bfloat16),
        ],
        scratch_shapes=[
            pltpu.VMEM((SLOTS, BLOCK, BLOCK), jnp.int32),
            pltpu.VMEM((SLOTS, BLOCK, BLOCK), jnp.bfloat16),
            pltpu.VMEM((NREL, WIDTH, WIDTH), jnp.bfloat16),
            pltpu.VMEM((NREL, WIDTH, WIDTH), jnp.bfloat16),
            pltpu.VMEM((NREL * NBLK, BLOCK), jnp.float32),
            pltpu.SemaphoreType.DMA((2 * CHUNKS + 2,)),
        ],
        compiler_params=params(52),
        cost_estimate=pl.CostEstimate(flops=2 * SLOTS * BLOCK * BLOCK * 8, bytes_accessed=12 * MIB, transcendentals=0),
        name="prep",
    )(codes, counts, rel_weight)


HALF_BLOCKS = NBLK // 2
HID = (NREL, NBLK, WIDTH, BLOCK)


def slot_pairs(codes_ref, pairs_ref, which, hid_ref, w_ref, acc_ref):
    def some(q, carry):
        for u in range(UNROLL):
            k = q * UNROLL + u
            s1, s2, place = pairs_ref[which, 0, k], pairs_ref[which, 1, k], pairs_ref[which, 2, k]
            hs = []
            for s in (s1, s2):
                code = codes_ref[s]
                hs.append(hid_ref[lax.shift_right_logical(code, 10), jnp.bitwise_and(code, NBLK - 1)])
            h = jnp.concatenate(hs, axis=1)
            w = jnp.concatenate([w_ref[s1], w_ref[s2]], axis=1)
            acc_ref[place] += lax.dot_general(h, w, NT, preferred_element_type=jnp.float32)
        return carry

    lax.fori_loop(0, pairs_ref[which, 3, 0], some, 0)


STEPS = NODES // CHUNK
PER_STEP = SLOTS // STEPS


def load_kernel(*refs):
    deg_refs, (place_ref, x_ref, wt_hbm, cnt_hbm, wt_ref, cnt_ref, inv_ref, hid, sems) = refs[:8], refs[8:]
    copies = [pltpu.make_async_copy(wt_hbm.at[r], wt_ref.at[r], sems.at[r]) for r in range(NREL)]
    copies.append(pltpu.make_async_copy(cnt_hbm, cnt_ref, sems.at[NREL]))
    for copy in copies:
        copy.start()
    degree = deg_refs[0][...].astype(jnp.float32)
    for ref in deg_refs[1:]:
        degree = degree + ref[...].astype(jnp.float32)
    inv_ref[...] = (1.0 / jnp.maximum(degree, 1.0)).T
    def step(i, carry, wait=False):
        first = place_ref[CORE] * HALF_BLOCKS + i * (CHUNK // BLOCK)
        x = x_ref[:, pl.ds(pl.multiple_of(i * CHUNK, CHUNK), CHUNK)]
        for r in range(NREL):
            if wait:
                copies[r].wait()
            h = jnp.dot(wt_ref[r], x, preferred_element_type=jnp.float32).astype(jnp.bfloat16)
            for b in range(CHUNK // BLOCK):
                hid[r, first + b] = h[:, b * BLOCK : (b + 1) * BLOCK]
        return carry

    step(0, 0, wait=True)
    lax.fori_loop(1, STEPS // 2, step, 0)
    copies[NREL].wait()


def load(degrees, place, x_mine, wt, cnt):
    return pl.pallas_call(
        load_kernel,
        in_specs=[VMEM_SPEC] * 8 + [SMEM_SPEC, VMEM_SPEC] + [ANY_SPEC] * 2,
        out_specs=[VMEM_SPEC] * 4,
        out_shape=[
            pltpu.VMEM(wt.shape, wt.dtype),
            pltpu.VMEM(cnt.shape, cnt.dtype),
            pltpu.VMEM((BLOCK, NREL * NBLK), jnp.float32),
            pltpu.VMEM(HID, jnp.bfloat16),
        ],
        scratch_shapes=[pltpu.SemaphoreType.DMA((NREL + 1,))],
        compiler_params=params(28),
        cost_estimate=pl.CostEstimate(flops=NODES * WIDTH * WIDTH * NREL, bytes_accessed=12 * MIB, transcendentals=0),
        name="own_hidden",
    )(*degrees, place, *here(x_mine), wt, cnt)


def here(*arrays):
    return [pltpu.with_memory_space_constraint(a, pltpu.VMEM) for a in arrays]


def sibling_kernel(place_ref, codes_ref, pairs_ref, inv_ref, x_ref, wt, cnt, hid_in, sib_ref, hid, w, acc):
    core = place_ref[CORE]
    w[SLOTS] = jnp.zeros((BLOCK, BLOCK), jnp.bfloat16)
    per_step = 2 * PER_STEP
    clear = 2 * HALF_BLOCKS // STEPS

    def step(i, carry):
        first = (1 - core) * HALF_BLOCKS + i * (CHUNK // BLOCK)
        x = x_ref[:, pl.ds(pl.multiple_of(i * CHUNK, CHUNK), CHUNK)]
        for r in range(NREL):
            h = jnp.dot(wt[r], x, preferred_element_type=jnp.float32).astype(jnp.bfloat16)
            for u in range(r * per_step // NREL, (r + 1) * per_step // NREL):
                slot = i * per_step + u
                seg = lax.shift_right_logical(codes_ref[slot], 5)
                factor = jnp.take_along_axis(inv_ref[...], jnp.full((BLOCK, BLOCK), seg, jnp.int32), axis=1)
                w[slot] = (cnt[slot].astype(jnp.float32) * factor).astype(jnp.bfloat16)
            for b in range(CHUNK // BLOCK):
                hid[r, first + b] = h[:, b * BLOCK : (b + 1) * BLOCK]
        for t in range(clear):
            acc[i * clear + t] = jnp.zeros((WIDTH, BLOCK), jnp.float32)
        return carry

    lax.fori_loop(0, STEPS // 2, step, 0)
    slot_pairs(codes_ref, pairs_ref, 0, hid, w, acc)

    def one(t, carry):
        sib_ref[t] = acc[t].astype(jnp.bfloat16)
        return carry

    lax.fori_loop(0, HALF_BLOCKS, one, 0)


def sibling_part(place, codes, pairs, inverse, x_other, wt, cnt, hid):
    return pl.pallas_call(
        sibling_kernel,
        in_specs=[SMEM_SPEC] * 3 + [VMEM_SPEC] * 5,
        out_specs=[VMEM_SPEC] * 3,
        out_shape=[
            pltpu.VMEM((HALF_BLOCKS, WIDTH, BLOCK), jnp.bfloat16),
            pltpu.VMEM(HID, jnp.bfloat16),
            pltpu.VMEM((SLOTS + 1, BLOCK, BLOCK), jnp.bfloat16),
        ],
        input_output_aliases={7: 1},
        scratch_shapes=[pltpu.VMEM((HALF_BLOCKS, WIDTH, BLOCK), jnp.float32)],
        compiler_params=params(12),
        cost_estimate=pl.CostEstimate(flops=2 * NODES * WIDTH * WIDTH * NREL, bytes_accessed=20 * MIB, transcendentals=0),
        name="sibling_part",
    )(place, codes, pairs, *here(inverse, x_other, wt, cnt, hid))


def own_kernel(place_ref, codes_ref, pairs_ref, xm_ref, xo_ref, self_ref, hid, w, own_ref):
    core = place_ref[CORE]

    @pl.when(place_ref[DIAGONAL] == 0)
    def _():
        def one(t, carry):
            own_ref[t] = jnp.zeros((WIDTH, BLOCK), jnp.float32)
            return carry

        lax.fori_loop(0, HALF_BLOCKS, one, 0)

    @pl.when(place_ref[DIAGONAL] == 1)
    def _():
        turned = self_ref[...].T
        for half, x_ref in ((core, xm_ref), (1 - core, xo_ref)):
            for q in range(HALF_BLOCKS // 4):
                at = pl.multiple_of(core * (2 * BLOCK) + q * (4 * BLOCK), 2 * BLOCK)
                term = jnp.dot(turned, x_ref[:, pl.ds(at, 2 * BLOCK)], preferred_element_type=jnp.float32)
                for b in range(2):
                    own_ref[half * (HALF_BLOCKS // 2) + q * 2 + b] = term[:, b * BLOCK : (b + 1) * BLOCK]

    slot_pairs(codes_ref, pairs_ref, 1, hid, w, own_ref)


def own_part(place, codes, pairs, x_mine, x_other, self_weight, hid, w):
    x_mine, x_other, hid, w = here(x_mine, x_other, hid, w)
    return pl.pallas_call(
        own_kernel,
        in_specs=[SMEM_SPEC] * 3 + [VMEM_SPEC] * 5,
        out_specs=VMEM_SPEC,
        out_shape=pltpu.VMEM((HALF_BLOCKS, WIDTH, BLOCK), jnp.float32),
        compiler_params=params(12),
        cost_estimate=pl.CostEstimate(flops=2 * HALF * WIDTH * WIDTH * NREL, bytes_accessed=20 * MIB, transcendentals=0),
        name="own_part",
    )(place, codes, pairs, x_mine, x_other, self_weight, hid, w)


def join_kernel(own_ref, other_ref, out_ref):
    per = out_ref.shape[0]
    step = pl.program_id(0)
    for t in range(per):
        out_ref[t] = (own_ref[step * per + t] + other_ref[t].astype(jnp.float32)).astype(jnp.bfloat16)


def join(own, other):
    spec = pl.BlockSpec((4, WIDTH, BLOCK), lambda i: (i, 0, 0))
    return pl.pallas_call(
        join_kernel,
        grid=(NBLK // 2 // 4,),
        in_specs=[VMEM_SPEC, spec],
        out_specs=spec,
        out_shape=jax.ShapeDtypeStruct((NBLK // 2, WIDTH, BLOCK), jnp.bfloat16),
        compiler_params=params(12),
        cost_estimate=pl.CostEstimate(flops=MIB, bytes_accessed=8 * MIB, transcendentals=0),
        name="join",
    )(own, other)


def finish_kernel(parts_ref, bias_ref, out_ref):
    for b in range(2):
        total = parts_ref[0, b].astype(jnp.float32)
        for k in range(1, parts_ref.shape[0]):
            total = total + parts_ref[k, b].astype(jnp.float32)
        rows = slice(b * BLOCK, (b + 1) * BLOCK)
        out_ref[rows, :] = jnp.maximum(total.T + bias_ref[...], 0.0).astype(jnp.bfloat16)


def finish(parts, bias):
    return pl.pallas_call(
        finish_kernel,
        out_shape=jax.ShapeDtypeStruct((2 * BLOCK, WIDTH), jnp.bfloat16),
        compiler_params=params(32),
        name="finish",
    )(parts, bias.reshape(1, WIDTH))


def pair_lists(codes, core):
    slots = jnp.arange(SLOTS, dtype=jnp.int32)
    target = codes // NBLK % NBLK
    half = (target // 2 % 2 == core).astype(jnp.int32)
    place = target // 4 * 2 + target % 2
    group = half * (NBLK // 2) + place
    same = group[None, :] == group[:, None]
    nth = jnp.sum((same & (slots[None, :] < slots[:, None])).astype(jnp.int32), axis=1)
    groups = jnp.arange(NBLK, dtype=jnp.int32)
    size = jnp.sum((group[None, :] == groups[:, None]).astype(jnp.int32), axis=1)
    need = (size + 1) // 2
    before = (groups[None, :] < groups[:, None]) & (groups[None, :] // (NBLK // 2) == groups[:, None] // (NBLK // 2))
    base = jnp.sum(jnp.where(before, need[None, :], 0), axis=1)
    at = half * PAIRS + nth // 2 + jnp.sum(jnp.where(group[:, None] == groups[None, :], base[None, :], 0), axis=1)
    entries = jnp.arange(2 * PAIRS, dtype=jnp.int32)
    match = at[None, :] == entries[:, None]
    is_first = match & (nth % 2 == 0)[None, :]
    is_second = match & (nth % 2 == 1)[None, :]
    first = SLOTS + jnp.sum(jnp.where(is_first, slots[None, :] - SLOTS, 0), axis=1)
    second = SLOTS + jnp.sum(jnp.where(is_second, slots[None, :] - SLOTS, 0), axis=1)
    where = jnp.sum(jnp.where(is_first, place[None, :], 0), axis=1)
    steps = (jnp.sum(need.reshape(2, NBLK // 2), axis=1) + UNROLL - 1) // UNROLL
    steps = jnp.broadcast_to(steps[:, None], (2, PAIRS))
    return jnp.stack([first.reshape(2, PAIRS), second.reshape(2, PAIRS), where.reshape(2, PAIRS), steps], axis=1)


def swap(array):
    return lax.ppermute(array, "rel", [(0, 1), (1, 0)])


def on_device(features, rel_weight, self_weight, bias, block_code, block_counts):
    row, col, core = lax.axis_index("rows"), lax.axis_index("cols"), lax.axis_index("rel")
    codes = block_code[0, 0, 0]
    counts = block_counts[0, 0, 0]

    x_half = lax.dynamic_slice(features.T, (0, core * HALF), (PIECE, HALF))
    x_sent = jnp.broadcast_to(x_half[None], (8, PIECE, HALF))
    x_sent, codes, core, row = lax.optimization_barrier((x_sent, codes, core, row))
    x_mine = lax.all_to_all(x_sent, "rows", 0, 0).reshape(WIDTH, HALF)

    padded = jnp.concatenate([codes, jnp.zeros((8,), jnp.int32)])
    place = jnp.stack([core, (row == col).astype(jnp.int32)]).astype(jnp.int32)
    pairs = pair_lists(codes, core)
    padded, place, pairs = lax.optimization_barrier((padded, place, pairs))
    deg_part, cnt, wt = prep(padded, counts, rel_weight)
    degrees = [deg_part] + [lax.ppermute(deg_part, "cols", [(i, (i + k) % 8) for i in range(8)]) for k in range(1, 8)]
    x_mine, cnt, wt, degrees = lax.optimization_barrier((x_mine, cnt, wt, degrees))

    x_other = swap(x_mine)
    wt, cnt, inverse, hid = load(degrees, place, x_mine, wt, cnt)
    to_sib, hid, w = sibling_part(place, padded, pairs, inverse, x_other, wt, cnt, hid)
    other = swap(to_sib)
    own = own_part(place, padded, pairs, x_mine, x_other, self_weight, hid, w)
    both = join(own, other)
    parts = lax.all_to_all(both.reshape(8, 2, WIDTH, BLOCK), "cols", 0, 0)
    return finish(parts, bias)


def solution(mesh):
    in_specs = (
        P("cols", "rows"),
        P("rel", None, None),
        P(),
        P(),
        P("rows", "cols", "rel", None),
        P("rows", "cols", "rel", None, None, None),
    )
    out_specs = P(("rows", "cols", "rel"), None)
    return jax.shard_map(on_device, mesh=mesh, in_specs=in_specs, out_specs=out_specs, check_vma=False)
```
